256 devices in a mesh: queue: 128 (over y, z, x_lo, core), heads: 2 (over x_hi).
Axes of the slice: x: 4 (x_hi: 2, x_lo: 2; x = x_hi * 2 + x_lo), y: 4, z: 8, core: 2. Of those that a mesh axis runs over, the one named last changes fastest.
Arguments:
- frames: bfloat16 [32768, 1536], P('queue', 'heads'), may hold values from -6 to 6
- fresh_groups: bfloat16 [3, 256, 1536], P(None, None, 'heads'), may hold values from -6 to 6
- level_index: int32 [128], replicated, may hold values from 0 to 63, as said below
- window_start: int32 [128], replicated, may hold values from 0 to 128
- mod_shift: bfloat16 [64, 1536], P(None, 'heads'), may hold values from -3 to 3
- mod_scale: bfloat16 [64, 1536], P(None, 'heads'), may hold values from -1.796875 to 1.796875
- mod_gate: bfloat16 [64, 1536], P(None, 'heads'), may hold values from -10 to 10
- w_qkv: bfloat16 [1536, 3, 1536], P(None, None, 'heads'), may hold values from -1 to 1
- q_gain: float32 [1536], P('heads'), may hold values from 0.5 to 5
- k_gain: float32 [1536], P('heads'), may hold values from 0.5 to 5
- w_out: bfloat16 [1536, 1536], P('heads'), may hold values from -0.5 to 0.5
Outputs:
- queue_state: bfloat16 [32768, 1536], P('queue', 'heads')
- last_velocity: bfloat16 [32768, 1536], P('queue', 'heads')
The draws below stay inside these ranges and needn't reach their ends.
Inputs may be any that keep to these rules, and one draw needn't show every extreme that they name: `level_index`: never falls from slot to slot; the first slot holds 0 and the last 63.
All inputs are finite; a program needn't handle non-finite values.
Results may differ from the reference program's by a relative error of at most 0.04.
Values may be sent and summed in bfloat16 or wider, within the bound.
No kernel may reach another device: no remote copies, remote signals or barrier semaphores. Data moves between devices by JAX's collectives and lax.ppermute only.
A program may use at most 128 MiB of HBM per device.

```python
import jax
import jax.numpy as jnp
from jax import lax

D = 1536
HEADS = 12
HD = 128
R = 256
STEPS = 3
LEVELS = 64
TOKENS = 32768
N_QUEUE = 128


def draw_level_index(key, part):
    key = jax.random.fold_in(key, 21)
    slots = jnp.arange(N_QUEUE, dtype=jnp.int32)
    base = slots * LEVELS // N_QUEUE + jax.random.randint(key, (N_QUEUE,), 0, 3, dtype=jnp.int32)
    rising = lax.cummax(base, axis=0)
    rising = jnp.clip(rising, 0, LEVELS - 1)
    return rising.at[0].set(0).at[N_QUEUE - 1].set(LEVELS - 1)


def draw_window_start(key, part):
    key = jax.random.fold_in(key, 22)
    starts = jax.random.randint(key, (N_QUEUE,), 0, R // 2 + 1, dtype=jnp.int32)
    return starts.at[1].set(0).at[2].set(R // 2)


def drawn_gains(key):
    return jnp.exp(jax.random.uniform(key, (HEADS * HD,), jnp.float32, jnp.log(0.7), jnp.log(1.6)))


def draw_q_gain(key, part):
    key = jax.random.fold_in(key, 23)
    return drawn_gains(key)


def draw_k_gain(key, part):
    key = jax.random.fold_in(key, 24)
    return drawn_gains(key)


def draw_frames(key, part):
    key = jax.random.fold_in(key, 25)
    base = jnp.clip(jax.random.normal(key, (TOKENS, D), jnp.float32), -6.0, 6.0)
    return base.astype(jnp.bfloat16)


def draw_w_qkv(key, part):
    key = jax.random.fold_in(key, 26)
    scale = 1.0 / jnp.sqrt(jnp.float32(D))
    base = jnp.clip(jax.random.normal(key, (D, 3, HEADS * HD), jnp.float32), -4.0, 4.0) * scale
    return base.astype(jnp.bfloat16)


def shard_levels(stream_key, shape, shards, smallest, high):
    def one(dim, parts):
        heights = jax.random.uniform(jax.random.fold_in(jax.random.fold_in(stream_key, 6), dim), (parts,), jnp.float32, smallest / len(shards), high / len(shards))
        return jnp.repeat(jnp.exp(heights), shape[dim] // parts).reshape((-1,) + (1,) * (len(shape) - dim - 1))

    factor_of = one(*shards[0])
    for cut in shards[1:]:
        factor_of = factor_of * one(*cut)
    return factor_of


def scatter_about(rng, extent, scale, limit, shards=(), kind=jnp.bfloat16):
    level = shard_levels(rng, extent, shards, -0.22, 0.18) if shards else 1.0
    result = jax.random.normal(rng, extent, jnp.float32) * scale * level
    return jnp.minimum(jnp.maximum(result, -limit), limit).astype(kind)


def setup_inputs(seed: int = 0) -> dict:
    key_list = jax.random.split(jax.random.key(seed), 12)
    frames = draw_frames(jax.random.fold_in(key_list[11], 71), 0)
    fresh_groups = scatter_about(key_list[1], (STEPS, R, D), 1.0, 6.0, ((2, 2),))
    level_index = draw_level_index(jax.random.fold_in(key_list[11], 71), 0)
    window_start = draw_window_start(jax.random.fold_in(key_list[11], 71), 0)
    mod_shift = scatter_about(key_list[4], (LEVELS, D), 0.5, 3.0, ((1, 2),))
    mod_scale = scatter_about(key_list[5], (LEVELS, D), 0.3, 1.796875, ((1, 2),))
    mod_gate = scatter_about(key_list[6], (LEVELS, D), 2.0, 10.0, ((1, 2),))
    w_qkv = draw_w_qkv(jax.random.fold_in(key_list[11], 71), 0)
    q_gain = draw_q_gain(jax.random.fold_in(key_list[11], 71), 0)
    k_gain = draw_k_gain(jax.random.fold_in(key_list[11], 71), 0)
    w_out = scatter_about(key_list[10], (HEADS * HD, D), HD ** -0.5, 0.5, ((0, 2),))
    return {"frames": frames, "fresh_groups": fresh_groups, "level_index": level_index, "window_start": window_start, "mod_shift": mod_shift, "mod_scale": mod_scale, "mod_gate": mod_gate, "w_qkv": w_qkv, "q_gain": q_gain, "k_gain": k_gain, "w_out": w_out}


def time_of(level):
    return (level.astype(jnp.float32) + 1.0) / LEVELS

def modulate(group, shift_row, scale_row):
    values = group.astype(jnp.float32)
    spread = jnp.sqrt(lax.optimization_barrier(jnp.mean(values * values, axis=-1, keepdims=True)) + 1e-06)
    return (values / spread * (1.0 + scale_row.astype(jnp.float32)) + shift_row.astype(jnp.float32)).astype(jnp.bfloat16)

def head_norm(block, gain):
    shaped = block.reshape(block.shape[0], -1, HD)
    spread = jnp.sqrt(lax.optimization_barrier(jnp.mean(shaped * shaped, axis=-1, keepdims=True)) + 1e-06)
    return ((shaped / spread).reshape(block.shape) * gain).astype(jnp.bfloat16)

def attend(query, keys, values, near_keys, near_values, start, alive):
    rows = query.shape[0]
    heads = query.shape[1] // HD
    qh = query.reshape(rows, heads, HD).astype(jnp.float32)
    own = jnp.einsum('rhe,she->hrs', qh, keys.reshape(rows, heads, HD).astype(jnp.float32)) / jnp.sqrt(jnp.float32(HD))
    near = jnp.einsum('rhe,she->hrs', qh, near_keys.reshape(rows, heads, HD).astype(jnp.float32)) / jnp.sqrt(jnp.float32(HD))
    visible = (jnp.arange(rows, dtype=jnp.int32) >= start) & alive
    near = jnp.where(visible[None, None, :], near, jnp.float32(-1e+30))
    top = jnp.maximum(lax.optimization_barrier(jnp.max(own, axis=-1, keepdims=True)), lax.optimization_barrier(jnp.max(near, axis=-1, keepdims=True)))
    own_exp = jnp.exp(own - top)
    near_exp = jnp.exp(near - top)
    total = lax.optimization_barrier(jnp.sum(own_exp, axis=-1, keepdims=True)) + lax.optimization_barrier(jnp.sum(near_exp, axis=-1, keepdims=True))
    own_w = (own_exp / total).astype(jnp.bfloat16).astype(jnp.float32)
    near_w = (near_exp / total).astype(jnp.bfloat16).astype(jnp.float32)
    out = jnp.einsum('hrs,she->rhe', own_w, values.reshape(rows, heads, HD).astype(jnp.float32))
    out = out + jnp.einsum('hrs,she->rhe', near_w, near_values.reshape(rows, heads, HD).astype(jnp.float32))
    return out.reshape(rows, heads * HD).astype(jnp.bfloat16)

def reference(frames, fresh_groups, level_index, window_start, mod_shift, mod_scale, mod_gate, w_qkv, q_gain, k_gain, w_out):
    width = w_qkv.shape[2]
    flat_weights = w_qkv.reshape(D, 3 * width)
    state = frames.reshape(N_QUEUE, R, D)
    slots = jnp.arange(N_QUEUE, dtype=jnp.int32)
    t_cur = time_of(level_index)
    below = level_index[jnp.maximum(slots - 1, 0)]
    t_next = jnp.where(slots > 0, time_of(below), jnp.float32(0.0))
    step_size = t_next - t_cur
    gates = mod_gate[level_index].astype(jnp.float32)
    velocity = jnp.zeros((N_QUEUE, R, D), jnp.float32)

    def project(item):
        group, level = item
        moved = modulate(group, mod_shift[level], mod_scale[level])
        qkv = jnp.dot(moved, flat_weights, preferred_element_type=jnp.float32).reshape(R, 3, width)
        return (head_norm(qkv[:, 0], q_gain), head_norm(qkv[:, 1], k_gain), qkv[:, 2].astype(jnp.bfloat16))
    for step in range(STEPS):
        query_all, key_all, value_all = lax.map(project, (state, level_index))
        key_near = jnp.concatenate([jnp.zeros_like(key_all[:1]), key_all[:-1]], axis=0)
        value_near = jnp.concatenate([jnp.zeros_like(value_all[:1]), value_all[:-1]], axis=0)

        def attend_slot(item):
            query, keys, values, near_keys, near_values, start, slot = item
            return attend(query, keys, values, near_keys, near_values, start, slot > 0)
        attended = lax.map(attend_slot, (query_all, key_all, value_all, key_near, value_near, window_start, slots))
        product = jnp.dot(attended.reshape(N_QUEUE * R, width), w_out, preferred_element_type=jnp.float32)
        velocity = gates[:, None, :] * product.reshape(N_QUEUE, R, D)
        updated = (state.astype(jnp.float32) + step_size[:, None, None] * velocity).astype(jnp.bfloat16)
        state = jnp.concatenate([updated[1:], fresh_groups[step][None]], axis=0)
    return (state.reshape(N_QUEUE * R, D), velocity.reshape(N_QUEUE * R, D).astype(jnp.bfloat16))
```

```python
import functools

import jax
import jax.numpy as jnp
from jax import lax
from jax.experimental import pallas as pl
from jax.experimental.pallas import tpu as pltpu
from jax.sharding import PartitionSpec as P

HD = 128
STEPS = 3
LEVELS = 64
EPS = 1e-06
AXES = ("queue", "heads")
VMEM_LIMIT = 56 * 1024 * 1024


def routed(block, target):
    slots, halves = lax.axis_size("queue"), lax.axis_size("heads")
    pairs = []
    for q in range(slots):
        for h in range(halves):
            q2, h2 = target(q, h)
            if 0 <= q2 < slots:
                pairs.append((q * halves + h, q2 * halves + h2))
    return lax.ppermute(block, AXES, pairs)


def modulated(x, shift, scale):
    values = x.astype(jnp.float32)
    mean = jnp.mean(values * values, axis=-1, keepdims=True)
    return (values * lax.rsqrt(mean + EPS) * (1.0 + scale) + shift).astype(jnp.bfloat16)


def normed(block, gain):
    mean = jnp.mean(block * block, axis=-1, keepdims=True)
    return (block * lax.rsqrt(mean + EPS) * gain).astype(jnp.bfloat16)


def dot(a, b):
    return jnp.dot(a, b, preferred_element_type=jnp.float32)


def dot_t(a, b):
    return lax.dot_general(a, b, (((1,), (1,)), ((), ())), preferred_element_type=jnp.float32)


def near_kernel(x, table, w, k_gain, keys, values):
    width = w.shape[2]
    moved = modulated(x[...], table[3:4, :], table[4:5, :])
    raw = dot(moved, w[1])
    for a in range(0, width, HD):
        keys[:, a : a + HD] = normed(raw[:, a : a + HD], k_gain[:, a : a + HD])
    values[...] = dot(moved, w[2]).astype(jnp.bfloat16)


def own_kernel(start, x, table, w, w_out, q_gain, k_gain, near_keys, near_values, term, attended):
    rows = x.shape[0]
    width = w.shape[2]
    moved = modulated(x[...], table[0:1, :], table[1:2, :])
    visible = lax.broadcasted_iota(jnp.int32, (1, rows), 1) >= start[0]
    factor = 1.4426950408889634 / (HD**0.5)
    query_raw = dot(moved, w[0])
    key_raw = dot(moved, w[1])
    value = dot(moved, w[2]).astype(jnp.bfloat16)
    for a in range(0, width, HD):
        part = slice(a, a + HD)
        query = normed(query_raw[:, part], q_gain[:, part])
        key = normed(key_raw[:, part], k_gain[:, part])
        own = dot_t(query, key)
        near = jnp.where(visible, dot_t(query, near_keys[:, part]), jnp.float32(-1e30))
        top = jnp.maximum(
            jnp.max(own, axis=-1, keepdims=True), jnp.max(near, axis=-1, keepdims=True)
        )
        own = jnp.exp2((own - top) * factor)
        near = jnp.exp2((near - top) * factor)
        total = jnp.sum(own, axis=-1, keepdims=True) + jnp.sum(near, axis=-1, keepdims=True)
        out = dot(own.astype(jnp.bfloat16), value[:, part])
        out = out + dot(near.astype(jnp.bfloat16), near_values[:, part])
        attended[:, part] = (out / total).astype(jnp.bfloat16)
    term[...] = dot(attended[...], w_out[...]).astype(jnp.bfloat16)


def whole_specs(count):
    return [pl.BlockSpec(memory_space=pltpu.VMEM)] * count


def near_call(x, table, w, k_gain):
    rows, width = x.shape[0], w.shape[2]
    out = jax.ShapeDtypeStruct((rows, width), jnp.bfloat16)
    return pl.pallas_call(
        near_kernel,
        out_shape=(out, out),
        in_specs=whole_specs(4),
        out_specs=tuple(whole_specs(2)),
        compiler_params=pltpu.CompilerParams(vmem_limit_bytes=VMEM_LIMIT),
    )(x, table, w, k_gain)


def own_call(start, x, table, w, w_out, q_gain, k_gain, near_keys, near_values):
    rows, width = x.shape[0], w.shape[2]
    return pl.pallas_call(
        own_kernel,
        out_shape=jax.ShapeDtypeStruct((rows, w_out.shape[1]), jnp.bfloat16),
        in_specs=[pl.BlockSpec(memory_space=pltpu.SMEM)] + whole_specs(8),
        out_specs=whole_specs(1)[0],
        scratch_shapes=[pltpu.VMEM((rows, width), jnp.bfloat16)],
        compiler_params=pltpu.CompilerParams(vmem_limit_bytes=VMEM_LIMIT),
    )(start, x, table, w, w_out, q_gain, k_gain, near_keys, near_values)


def on_device(
    frames,
    fresh_groups,
    level_index,
    window_start,
    mod_shift,
    mod_scale,
    mod_gate,
    w_qkv,
    q_gain,
    k_gain,
    w_out,
):
    position = lax.axis_index("queue")
    half = lax.axis_index("heads")
    slot_count = lax.axis_size("queue")
    rows = frames.shape[0]
    features = frames.shape[1]
    level = level_index[position]
    below = level_index[jnp.maximum(position - 1, 0)]
    t_cur = (level.astype(jnp.float32) + 1.0) / LEVELS
    t_next = jnp.where(position > 0, (below.astype(jnp.float32) + 1.0) / LEVELS, jnp.float32(0.0))
    step_size = t_next - t_cur
    start = jnp.where(position > 0, window_start[position], rows).astype(jnp.int32).reshape(1)
    w = jnp.transpose(w_qkv, (1, 0, 2))
    q_gain = q_gain.reshape(1, -1)
    k_gain = k_gain.reshape(1, -1)

    def swap(block):
        return routed(block, lambda q, h: (q, 1 - h))

    def up(block):
        return routed(block, lambda q, h: (q + 1, h))

    def down(block):
        return routed(block, lambda q, h: (q - 1, h))

    def both(mine, other):
        return jnp.where(
            half == 0,
            jnp.concatenate([mine, other], axis=-1),
            jnp.concatenate([other, mine], axis=-1),
        )

    table_rows = [mod_shift[level], mod_scale[level], mod_gate[level], mod_shift[below], mod_scale[below]]
    my_rows = jnp.stack(table_rows + [jnp.zeros_like(table_rows[0])] * 11)
    near_mine = up(frames)
    send = jnp.concatenate([frames, my_rows], axis=0)
    received = swap(send)
    near_other = up(received[:rows])
    state = both(frames, received[:rows])
    table = both(my_rows, received[rows:]).astype(jnp.float32)
    near = both(near_mine, near_other)
    last = slot_count - 1
    fresh_sent = fresh_groups[: STEPS - 1]
    fresh_other = lax.ppermute(fresh_sent, AXES, [(2 * last, 2 * last + 1), (2 * last + 1, 2 * last)])
    fresh = both(fresh_sent, fresh_other)
    gate = table[2:3]
    for step in range(STEPS):
        near_keys, near_values = near_call(near, table, w, k_gain)
        term = own_call(start, state, table, w, w_out, q_gain, k_gain, near_keys, near_values)
        if step < STEPS - 1:
            other = swap(term)
            velocity = gate * (term.astype(jnp.float32) + other.astype(jnp.float32))
            near = (state.astype(jnp.float32) + step_size * velocity).astype(jnp.bfloat16)
            advanced = down(near)
            state = jnp.where(position == last, fresh[step], advanced)
        else:
            low, high = term[:, :features], term[:, features:]
            other = swap(jnp.where(half == 0, high, low))
            mine = jnp.where(half == 0, low, high)
            gate = my_rows[2:3].astype(jnp.float32)
            velocity = gate * (mine.astype(jnp.float32) + other.astype(jnp.float32))
            held = jnp.where(half == 0, state[:, :features], state[:, features:])
            updated = (held.astype(jnp.float32) + step_size * velocity).astype(jnp.bfloat16)
            advanced = down(updated)
            state = jnp.where(position == last, fresh_groups[step], advanced)
    return (state, velocity.astype(jnp.bfloat16))


def solution(mesh):
    placed = (
        P("queue", "heads"),
        P(None, None, "heads"),
        P(),
        P(),
        P(None, "heads"),
        P(None, "heads"),
        P(None, "heads"),
        P(None, None, "heads"),
        P("heads"),
        P("heads"),
        P("heads", None),
    )
    return jax.shard_map(
        on_device,
        mesh=mesh,
        in_specs=placed,
        out_specs=(P("queue", "heads"), P("queue", "heads")),
        check_vma=False,
    )
```

```python
import functools

import jax
import jax.numpy as jnp
from jax import lax
from jax.experimental import pallas as pl
from jax.experimental.pallas import tpu as pltpu
from jax.sharding import PartitionSpec as P

HD = 128
STEPS = 3
LEVELS = 64
EPS = 1e-06
AXES = ("queue", "heads")
VMEM_LIMIT = 24 * 1024 * 1024
CHUNKS = 2
SHIFT, SCALE, GATE, NEAR_SHIFT, NEAR_SCALE = range(5)
TABLE_ROWS = 16


def routed(block, target):
    slots, halves = lax.axis_size("queue"), lax.axis_size("heads")
    pairs = []
    for q in range(slots):
        for h in range(halves):
            to = target(q, h)
            if to is not None and 0 <= to[0] < slots:
                pairs.append((q * halves + h, to[0] * halves + to[1]))
    return lax.ppermute(block, AXES, pairs)


def dot(a, b):
    return jnp.dot(a, b, preferred_element_type=jnp.float32)


def dot_t(a, b):
    return lax.dot_general(a, b, (((1,), (1,)), ((), ())), preferred_element_type=jnp.float32)


def modulated(low, high, shift, scale):
    low, high = low.astype(jnp.float32), high.astype(jnp.float32)
    total = jnp.sum(low * low, axis=-1, keepdims=True) + jnp.sum(high * high, axis=-1, keepdims=True)
    factor = lax.rsqrt(total / (2 * low.shape[-1]) + EPS)
    parts = [low, high]
    for n in range(2):
        parts[n] = (parts[n] * factor * (1.0 + scale[n]) + shift[n]).astype(jnp.bfloat16)
    return jnp.concatenate(parts, axis=-1)


def normed(block, gain):
    mean = jnp.mean(block * block, axis=-1, keepdims=True)
    return (block * lax.rsqrt(mean + EPS) * gain).astype(jnp.bfloat16)


def ordered(mine, other):
    first = lax.axis_index("heads") == 0
    return jnp.where(first, mine, other), jnp.where(first, other, mine)


def table_row(rows, n):
    mine, other = (r[n : n + 1, :].astype(jnp.float32) for r in rows)
    return ordered(mine, other)


def halves_of(kind, refs, step, row, count):
    if kind == "pair":
        return ordered(refs[0][row : row + count, :], refs[1][row : row + count, :])
    fresh, fresh_other, *chunks = refs
    size = chunks[0].shape[0]
    wide = [c[...] for c in chunks[row // size : (row + count) // size]]
    wide = wide[0] if len(wide) == 1 else jnp.concatenate(wide, axis=0)
    width = wide.shape[1] // 2
    low, high = wide[:, :width], wide[:, width:]
    if kind == "chunks":
        return low, high
    passed = ordered(fresh[step, row : row + count, :], fresh_other[step, row : row + count, :])
    last = lax.axis_index("queue") == lax.axis_size("queue") - 1
    return jnp.where(last, passed[0], low), jnp.where(last, passed[1], high)


def rows_kernel(levels, shift_hbm, scale_hbm, gate_hbm, rows, shift, scale, gate, arrived):
    tables = ((shift_hbm, shift), (scale_hbm, scale), (gate_hbm, gate))
    copies = [pltpu.make_async_copy(a, b, arrived.at[n]) for n, (a, b) in enumerate(tables)]
    for copy in copies:
        copy.start()
    position = lax.axis_index("queue")
    level = levels[position]
    below = levels[jnp.maximum(position - 1, 0)]
    shape = (TABLE_ROWS, shift.shape[0])
    row = lax.broadcasted_iota(jnp.int32, shape, 0)
    column = lax.broadcasted_iota(jnp.int32, shape, 1)

    def picked(table, own, near):
        chosen = jnp.logical_and(row == own, column == level)
        if near is not None:
            chosen = jnp.logical_or(chosen, jnp.logical_and(row == near, column == below))
        return dot(jnp.where(chosen, 1.0, 0.0).astype(jnp.bfloat16), table[...])

    for copy in copies:
        copy.wait()
    out = picked(shift, SHIFT, NEAR_SHIFT) + picked(scale, SCALE, NEAR_SCALE)
    rows[...] = (out + picked(gate, GATE, None)).astype(jnp.bfloat16)


def rows_call(levels, tables):
    held = [pltpu.VMEM(table.shape, table.dtype) for table in tables]
    return pl.pallas_call(
        rows_kernel,
        out_shape=jax.ShapeDtypeStruct((TABLE_ROWS, tables[0].shape[1]), jnp.bfloat16),
        in_specs=[pl.BlockSpec(memory_space=pltpu.SMEM)] + [pl.BlockSpec(memory_space=pltpu.HBM)] * len(tables),
        out_specs=pl.BlockSpec(memory_space=pltpu.VMEM),
        scratch_shapes=held + [pltpu.SemaphoreType.DMA((len(tables),))],
        compiler_params=pltpu.CompilerParams(vmem_limit_bytes=VMEM_LIMIT),
    )(levels, *(pltpu.with_memory_space_constraint(table, pltpu.HBM) for table in tables))


def stage_kernel(w_hbm, w_out_hbm, q_gain, k_gain, w, w_out, gains, arrived):
    copies = [pltpu.make_async_copy(w_hbm, w, arrived.at[0]), pltpu.make_async_copy(w_out_hbm, w_out, arrived.at[1])]
    for copy in copies:
        copy.start()
    gains[0:1, :] = q_gain[...].reshape(1, -1)
    gains[1:2, :] = k_gain[...].reshape(1, -1)
    for copy in copies:
        copy.wait()


def stage_call(w, w_out, q_gain, k_gain):
    vmem = pl.BlockSpec(memory_space=pltpu.VMEM)
    held = [pltpu.with_memory_space_constraint(a, pltpu.HBM) for a in (w, w_out)]
    return pl.pallas_call(
        stage_kernel,
        out_shape=(
            pltpu.VMEM(w.shape, w.dtype),
            pltpu.VMEM(w_out.shape, w_out.dtype),
            pltpu.VMEM((2, q_gain.shape[0]), q_gain.dtype),
        ),
        in_specs=[pl.BlockSpec(memory_space=pl.ANY)] * 2 + [vmem] * 2,
        out_specs=(vmem, vmem, vmem),
        scratch_shapes=[pltpu.SemaphoreType.DMA((2,))],
        compiler_params=pltpu.CompilerParams(vmem_limit_bytes=VMEM_LIMIT),
    )(*held, q_gain, k_gain)


def near_kernel(kind, rows_mine, rows_other, w, gains, *refs):
    x, (keys, values) = refs[:-2], refs[-2:]
    width = w.shape[2]
    table = (rows_mine, rows_other)
    low, high = halves_of(kind, x, None, 0, keys.shape[0])
    moved = modulated(low, high, table_row(table, NEAR_SHIFT), table_row(table, NEAR_SCALE))
    raw = dot(moved, w[1])
    gain = gains[1:2, :]
    for a in range(0, width, HD):
        keys[:, a : a + HD] = normed(raw[:, a : a + HD], gain[:, a : a + HD])
    values[...] = dot(moved, w[2]).astype(jnp.bfloat16)


def attend(starts, query, key, value, near_key, near_value):
    position = lax.axis_index("queue")
    start = jnp.where(position > 0, starts[position], near_key.shape[0])
    visible = lax.broadcasted_iota(jnp.int32, (1, near_key.shape[0]), 1) >= start
    factor = 1.4426950408889634 / (HD**0.5)
    own = dot_t(query, key)
    near = jnp.where(visible, dot_t(query, near_key), jnp.float32(-1e30))
    top = jnp.maximum(jnp.max(own, axis=-1, keepdims=True), jnp.max(near, axis=-1, keepdims=True))
    own = jnp.exp2((own - top) * factor)
    near = jnp.exp2((near - top) * factor)
    total = jnp.sum(own, axis=-1, keepdims=True) + jnp.sum(near, axis=-1, keepdims=True)
    out = dot(own.astype(jnp.bfloat16), value) + dot(near.astype(jnp.bfloat16), near_value)
    return (out / total).astype(jnp.bfloat16)


def own_kernel(kind, step, count, starts, rows_mine, rows_other, w, gains, near_keys, near_values, *refs):
    x, (attended, queries, keys, values) = refs[:-4], refs[-4:]
    rows = keys.shape[0]
    width = w.shape[2]
    first = attended.shape[0]
    table = (rows_mine, rows_other)
    low, high = halves_of(kind, x, step, 0, rows)
    moved = modulated(low, high, table_row(table, SHIFT), table_row(table, SCALE))
    query_raw = dot(moved, w[0])
    key_raw = dot(moved, w[1])
    value = dot(moved, w[2]).astype(jnp.bfloat16)
    values[...] = value
    q_row, k_row = gains[0:1, :], gains[1:2, :]
    for a in range(0, width, HD):
        part = slice(a, a + HD)
        query = normed(query_raw[:, part], q_row[:, part])
        key = normed(key_raw[:, part], k_row[:, part])
        queries[:, part] = query[first:]
        keys[:, part] = key
        attended[:, part] = attend(
            starts, query[:first], key, value[:, part], near_keys[:, part], near_values[:, part]
        )


def qkv_kernel(kind, rows_mine, rows_other, w, gains, *refs):
    x, (*queries, keys, values) = refs[:2], refs[2:]
    rows = keys.shape[0]
    width = w.shape[2]
    table = (rows_mine, rows_other)
    low, high = halves_of(kind, x, None, 0, rows)
    moved = modulated(low, high, table_row(table, SHIFT), table_row(table, SCALE))
    query_raw = dot(moved, w[0])
    key_raw = dot(moved, w[1])
    values[...] = dot(moved, w[2]).astype(jnp.bfloat16)
    q_row, k_row = gains[0:1, :], gains[1:2, :]
    for a in range(0, width, HD):
        part = slice(a, a + HD)
        query = normed(query_raw[:, part], q_row[:, part])
        keys[:, part] = normed(key_raw[:, part], k_row[:, part])
        for n, chunk in enumerate(queries):
            chunk[:, part] = query[n * chunk.shape[0] : (n + 1) * chunk.shape[0]]


def rest_kernel(starts, queries, keys, values, near_keys, near_values, attended):
    for a in range(0, attended.shape[1], HD):
        part = slice(a, a + HD)
        attended[:, part] = attend(
            starts, queries[:, part], keys[:, part], values[:, part], near_keys[:, part], near_values[:, part]
        )


def step_size_of(levels):
    position = lax.axis_index("queue")
    level = levels[position]
    below = levels[jnp.maximum(position - 1, 0)]
    t_cur = (level.astype(jnp.float32) + 1.0) / LEVELS
    t_next = jnp.where(position > 0, (below.astype(jnp.float32) + 1.0) / LEVELS, jnp.float32(0.0))
    return t_next - t_cur


def project_kernel(kind, step, row, levels, rows_mine, rows_other, w_mine, w_other, a_mine, a_other, *refs):
    x, new = refs[:-1], refs[-1]
    count = new.shape[0]
    width = new.shape[1] // 2
    gate = table_row((rows_mine, rows_other), GATE)
    halves = halves_of(kind, x, step - 1, row, count)
    product = dot(a_mine[...], w_mine[...]) + dot(a_other[...], w_other[...])
    for n in range(2):
        part = slice(n * width, (n + 1) * width)
        velocity = gate[n] * product[:, part]
        value = (halves[n].astype(jnp.float32) + step_size_of(levels) * velocity).astype(jnp.bfloat16)
        new[:, part] = value


def final_kernel(kind, step, row, levels, rows_mine, w_mine, w_other, a_mine, a_other, *refs):
    x, (new, velocity_out) = refs[:-2], refs[-2:]
    count, width = new.shape
    half = lax.axis_index("heads")
    part = pl.ds(pl.multiple_of(half * width, HD), width)
    low, high = halves_of(kind, x, step - 1, row, count)
    held = jnp.where(half == 0, low, high).astype(jnp.float32)
    product = dot(a_mine[...], w_mine[:, part]) + dot(a_other[...], w_other[:, part])
    velocity = rows_mine[GATE : GATE + 1, :].astype(jnp.float32) * product
    velocity_out[...] = velocity.astype(jnp.bfloat16)
    new[...] = (held + step_size_of(levels) * velocity).astype(jnp.bfloat16)


def piece_of(position):
    core = position % 2
    z = (position // 4) % 8
    y = position // 32
    return (y + 2 * z) % 4, core


def gather_kernel(own, back, ahead, across, others, w_other):
    group, core = piece_of(lax.axis_index("queue"))
    size = own.shape[0]
    for n, (block, turn) in enumerate(((own, 0), (back, 3), (ahead, 1), (across, 2))):
        place = (group + turn) % 4 * 2
        w_other[pl.ds(pl.multiple_of((place + core) * size, 16), size), :] = block[...]
        w_other[pl.ds(pl.multiple_of((place + 1 - core) * size, 16), size), :] = others[n]


def kernel_call(kernel, out, scalars, arrays, products=0, exponentials=0, dtype=jnp.bfloat16):
    many = isinstance(out[0], tuple)
    outs = out if many else (out,)
    shapes = tuple(jax.ShapeDtypeStruct(s, dtype) for s in outs)
    size = sum(a.size * a.dtype.itemsize for a in arrays)
    result = pl.pallas_call(
        kernel,
        cost_estimate=pl.CostEstimate(
            flops=2 * products, bytes_accessed=size, transcendentals=exponentials
        ),
        out_shape=shapes,
        in_specs=[pl.BlockSpec(memory_space=pltpu.SMEM)] * len(scalars)
        + [pl.BlockSpec(memory_space=pltpu.VMEM)] * len(arrays),
        out_specs=tuple([pl.BlockSpec(memory_space=pltpu.VMEM)] * len(outs)),
        compiler_params=pltpu.CompilerParams(vmem_limit_bytes=VMEM_LIMIT),
    )(*scalars, *arrays)
    return result if many else result[0]


def after(block, *others):
    return lax.optimization_barrier((block, *others))[0]


def fetched_piece(w_out):
    size = w_out.shape[0] // 8
    group, core = piece_of(lax.axis_index("queue"))
    return lax.dynamic_slice_in_dim(w_out, (group * 2 + core) * size, size, 0)


def other_projection(own, ready, shape):
    def turned(y, z):
        return lambda q, h: ((q // 32 + y) % 4 * 32 + (q // 4 + z) % 8 * 4 + q % 4, h)

    back = routed(own, turned(1, 0))
    ahead = routed(own, turned(-1, 0))
    across = routed(own, turned(0, 1))
    own, back, ahead, across, _ = lax.optimization_barrier((own, back, ahead, across, ready))
    others = routed(jnp.stack([own, back, ahead, across]), lambda q, h: (q ^ 1, h))
    return kernel_call(gather_kernel, shape, (), (own, back, ahead, across, others))


def on_device(
    frames,
    fresh_groups,
    level_index,
    window_start,
    mod_shift,
    mod_scale,
    mod_gate,
    w_qkv,
    q_gain,
    k_gain,
    w_out,
):
    position = lax.axis_index("queue")
    last = lax.axis_size("queue") - 1
    rows, width = frames.shape
    count = rows // CHUNKS
    w = jnp.transpose(w_qkv, (1, 0, 2))
    group_products = rows * w.shape[1] * width
    attention_products = 4 * count * rows * width
    out_products = 2 * count * width * width

    def swap(block):
        return routed(block, lambda q, h: (q, 1 - h))

    def up(block):
        return routed(block, lambda q, h: (q + 1, h))

    def down(block):
        return routed(block, lambda q, h: (q - 1, h))

    w_out_hbm = w_out
    other = swap(frames)
    rows_mine = rows_call(level_index, (mod_shift, mod_scale, mod_gate))
    rows_other = swap(rows_mine)
    w, w_out, gains = stage_call(w, w_out, q_gain, k_gain)
    near_mine = up(frames)
    near_other = up(after(other, rows_other, gains))
    piece = routed(fetched_piece(w_out_hbm), lambda q, h: (q ^ 2, 1 - h))
    table = (rows_mine, rows_other)
    kind, state = "pair", (frames, other)
    near_kind, near = "pair", (near_mine, near_other)
    *queries, keys, values = kernel_call(
        functools.partial(qkv_kernel, kind),
        ((count, width),) * CHUNKS + ((rows, width), (rows, width)),
        (),
        (*table, w, gains, *state),
        3 * group_products,
    )
    fresh_other = routed(
        after(fresh_groups[: STEPS - 1], other),
        lambda q, h: (last, 1 - h) if q == last - 2 else None,
    )
    near = (near_mine, after(near_other, keys, fresh_other))
    for step in range(STEPS):
        near_keys, near_values = kernel_call(
            functools.partial(near_kernel, near_kind),
            ((rows, width), (rows, width)),
            (),
            (*table, w, gains, *near),
            2 * group_products,
        )
        if step == 0:
            parts = []
        else:
            first, *queries, keys, values = kernel_call(
                functools.partial(own_kernel, kind, step - 1, count),
                ((count, width), (rows - count, width), (rows, width), (rows, width)),
                (window_start,),
                (*table, w, gains, near_keys, near_values, *state),
                3 * group_products + attention_products,
                attention_products // HD,
            )
            parts = [first]
        for query in queries:
            part = kernel_call(
                rest_kernel,
                (count, width),
                (window_start,),
                (after(query, *parts), keys, values, near_keys, near_values),
                attention_products,
                attention_products // HD,
            )
            parts.append(part)
        received = [swap(part) for part in parts]
        if step == 0:
            w_other = other_projection(after(piece, other, rows_other, near_mine), near_keys, w_out.shape)
        if step < STEPS - 1:
            new = []
            for n in range(CHUNKS):
                block = kernel_call(
                    functools.partial(project_kernel, kind, step, n * count),
                    (count, 2 * width),
                    (level_index,),
                    (*table, w_out, w_other, parts[n], after(received[n], *new), *state),
                    2 * out_products,
                )
                new.append(block)
            state = (fresh_groups, fresh_other, *[down(block) for block in new])
            near_kind, near = "chunks", (fresh_groups, fresh_other, *(after(block, state[2]) for block in new))
            kind = "fresh"
        else:
            done = []
            for n in range(CHUNKS):
                pair = kernel_call(
                    functools.partial(final_kernel, kind, step, n * count),
                    ((count, width), (count, width)),
                    (level_index,),
                    (rows_mine, w_out, w_other, parts[n], after(received[n], *(p[0] for p in done)), *state),
                    out_products,
                )
                done.append(pair)
            advanced = jnp.concatenate([down(block) for block, _ in done], axis=0)
            velocity = jnp.concatenate([block for _, block in done], axis=0)
            final = jnp.where(position == last, fresh_groups[step], advanced)
    return (final, velocity)


def solution(mesh):
    placed = (
        P("queue", "heads"),
        P(None, None, "heads"),
        P(),
        P(),
        P(None, "heads"),
        P(None, "heads"),
        P(None, "heads"),
        P(None, None, "heads"),
        P("heads"),
        P("heads"),
        P("heads", None),
    )
    return jax.shard_map(
        on_device,
        mesh=mesh,
        in_specs=placed,
        out_specs=(P("queue", "heads"), P("queue", "heads")),
        check_vma=False,
    )
```

```python
import functools

import jax
import jax.numpy as jnp
from jax import lax
from jax.experimental import pallas as pl
from jax.experimental.pallas import tpu as pltpu
from jax.sharding import PartitionSpec as P

HD = 128
STEPS = 3
LEVELS = 64
EPS = 1e-06
AXES = ("queue", "heads")
VMEM_LIMIT = 24 * 1024 * 1024
CHUNKS = 2
SHIFT, SCALE, GATE, NEAR_SHIFT, NEAR_SCALE = range(5)
TABLE_ROWS = 16


def routed(block, target):
    slots, halves = lax.axis_size("queue"), lax.axis_size("heads")
    pairs = []
    for q in range(slots):
        for h in range(halves):
            to = target(q, h)
            if to is not None and 0 <= to[0] < slots:
                pairs.append((q * halves + h, to[0] * halves + to[1]))
    return lax.ppermute(block, AXES, pairs)


def dot(a, b):
    return jnp.dot(a, b, preferred_element_type=jnp.float32)


def dot_t(a, b):
    return lax.dot_general(a, b, (((1,), (1,)), ((), ())), preferred_element_type=jnp.float32)


def modulated(low, high, shift, scale):
    low, high = low.astype(jnp.float32), high.astype(jnp.float32)
    total = jnp.sum(low * low, axis=-1, keepdims=True) + jnp.sum(high * high, axis=-1, keepdims=True)
    factor = lax.rsqrt(total / (2 * low.shape[-1]) + EPS)
    parts = [low, high]
    for n in range(2):
        parts[n] = (parts[n] * factor * (1.0 + scale[n]) + shift[n]).astype(jnp.bfloat16)
    return jnp.concatenate(parts, axis=-1)


def normed(block, gain):
    mean = jnp.mean(block * block, axis=-1, keepdims=True)
    return (block * lax.rsqrt(mean + EPS) * gain).astype(jnp.bfloat16)


def ordered(mine, other):
    first = lax.axis_index("heads") == 0
    return jnp.where(first, mine, other), jnp.where(first, other, mine)


def table_row(rows, n):
    mine, other = (r[n : n + 1, :].astype(jnp.float32) for r in rows)
    return ordered(mine, other)


def halves_of(kind, refs, step, row, count):
    if kind == "pair":
        return ordered(refs[0][row : row + count, :], refs[1][row : row + count, :])
    fresh, fresh_other, *chunks = refs
    size = chunks[0].shape[0]
    wide = [c[...] for c in chunks[row // size : (row + count) // size]]
    wide = wide[0] if len(wide) == 1 else jnp.concatenate(wide, axis=0)
    width = wide.shape[1] // 2
    low, high = wide[:, :width], wide[:, width:]
    if kind == "chunks":
        return low, high
    passed = ordered(fresh[step, row : row + count, :], fresh_other[step, row : row + count, :])
    last = lax.axis_index("queue") == lax.axis_size("queue") - 1
    return jnp.where(last, passed[0], low), jnp.where(last, passed[1], high)


def rows_kernel(levels_hbm, shift_hbm, scale_hbm, gate_hbm, rows, levels, shift, scale, gate, arrived):
    tables = ((levels_hbm, levels), (shift_hbm, shift), (scale_hbm, scale), (gate_hbm, gate))
    copies = [pltpu.make_async_copy(a, b, arrived.at[n]) for n, (a, b) in enumerate(tables)]
    for copy in copies:
        copy.start()
    for copy in copies:
        copy.wait()
    position = lax.axis_index("queue")
    level = levels[position]
    below = levels[jnp.maximum(position - 1, 0)]
    shape = (TABLE_ROWS, shift.shape[0])
    row = lax.broadcasted_iota(jnp.int32, shape, 0)
    column = lax.broadcasted_iota(jnp.int32, shape, 1)

    def picked(table, own, near):
        chosen = jnp.logical_and(row == own, column == level)
        if near is not None:
            chosen = jnp.logical_or(chosen, jnp.logical_and(row == near, column == below))
        return dot(jnp.where(chosen, 1.0, 0.0).astype(jnp.bfloat16), table[...])

    out = picked(shift, SHIFT, NEAR_SHIFT) + picked(scale, SCALE, NEAR_SCALE)
    rows[...] = (out + picked(gate, GATE, None)).astype(jnp.bfloat16)


def rows_call(levels, tables):
    held = [pltpu.VMEM(table.shape, table.dtype) for table in tables]
    return pl.pallas_call(
        rows_kernel,
        out_shape=jax.ShapeDtypeStruct((TABLE_ROWS, tables[0].shape[1]), jnp.bfloat16),
        in_specs=[pl.BlockSpec(memory_space=pl.ANY)] * (1 + len(tables)),
        out_specs=pl.BlockSpec(memory_space=pltpu.VMEM),
        scratch_shapes=[pltpu.SMEM(levels.shape, levels.dtype)] + held + [pltpu.SemaphoreType.DMA((1 + len(tables),))],
        compiler_params=pltpu.CompilerParams(vmem_limit_bytes=VMEM_LIMIT),
    )(*(pltpu.with_memory_space_constraint(a, pltpu.HBM) for a in (levels, *tables)))


def stage_kernel(w_hbm, q_hbm, k_hbm, fresh_hbm, w_out_hbm, w, gains, fresh, w_out, q_gain, k_gain, arrived):
    moves = (
        (w_hbm, w),
        (q_hbm, q_gain),
        (k_hbm, k_gain),
        (fresh_hbm.at[0 : STEPS - 1], fresh),
        (w_out_hbm, w_out),
    )
    copies = [pltpu.make_async_copy(a, b, arrived.at[n]) for n, (a, b) in enumerate(moves)]
    for copy in copies:
        copy.start()
    for copy in copies:
        copy.wait()
    gains[0:1, :] = q_gain[...].reshape(1, -1)
    gains[1:2, :] = k_gain[...].reshape(1, -1)


def stage_call(w, q_gain, k_gain, fresh, w_out):
    vmem = pl.BlockSpec(memory_space=pltpu.VMEM)
    held = [pltpu.with_memory_space_constraint(a, pltpu.HBM) for a in (w, q_gain, k_gain, fresh, w_out)]
    return pl.pallas_call(
        stage_kernel,
        out_shape=(
            pltpu.VMEM(w.shape, w.dtype),
            pltpu.VMEM((2, q_gain.shape[0]), q_gain.dtype),
            pltpu.VMEM((STEPS - 1, *fresh.shape[1:]), fresh.dtype),
            pltpu.VMEM(w_out.shape, w_out.dtype),
        ),
        in_specs=[pl.BlockSpec(memory_space=pl.ANY)] * 5,
        out_specs=(vmem, vmem, vmem, vmem),
        scratch_shapes=[
            pltpu.VMEM(q_gain.shape, q_gain.dtype),
            pltpu.VMEM(k_gain.shape, k_gain.dtype),
            pltpu.SemaphoreType.DMA((5,)),
        ],
        compiler_params=pltpu.CompilerParams(vmem_limit_bytes=VMEM_LIMIT),
    )(*held)


def near_kernel(kind, rows_mine, rows_other, w, gains, *refs):
    x, (keys, values) = refs[:-2], refs[-2:]
    width = w.shape[2]
    table = (rows_mine, rows_other)
    low, high = halves_of(kind, x, None, 0, keys.shape[0])
    moved = modulated(low, high, table_row(table, NEAR_SHIFT), table_row(table, NEAR_SCALE))
    raw = dot(moved, w[1])
    gain = gains[1:2, :]
    for a in range(0, width, HD):
        keys[:, a : a + HD] = normed(raw[:, a : a + HD], gain[:, a : a + HD])
    values[...] = dot(moved, w[2]).astype(jnp.bfloat16)


def attend(starts, query, key, value, near_key, near_value):
    position = lax.axis_index("queue")
    start = jnp.where(position > 0, starts[position], near_key.shape[0])
    visible = lax.broadcasted_iota(jnp.int32, (1, near_key.shape[0]), 1) >= start
    factor = 1.4426950408889634 / (HD**0.5)
    own = dot_t(query, key)
    near = jnp.where(visible, dot_t(query, near_key), jnp.float32(-1e30))
    top = jnp.maximum(jnp.max(own, axis=-1, keepdims=True), jnp.max(near, axis=-1, keepdims=True))
    own = jnp.exp2((own - top) * factor)
    near = jnp.exp2((near - top) * factor)
    total = jnp.sum(own, axis=-1, keepdims=True) + jnp.sum(near, axis=-1, keepdims=True)
    out = dot(own.astype(jnp.bfloat16), value) + dot(near.astype(jnp.bfloat16), near_value)
    return (out / total).astype(jnp.bfloat16)


def own_kernel(kind, step, count, starts, rows_mine, rows_other, w, gains, near_keys, near_values, *refs):
    x, (attended, queries, keys, values) = refs[:-4], refs[-4:]
    rows = keys.shape[0]
    width = w.shape[2]
    first = attended.shape[0]
    table = (rows_mine, rows_other)
    low, high = halves_of(kind, x, step, 0, rows)
    moved = modulated(low, high, table_row(table, SHIFT), table_row(table, SCALE))
    query_raw = dot(moved, w[0])
    key_raw = dot(moved, w[1])
    value = dot(moved, w[2]).astype(jnp.bfloat16)
    values[...] = value
    q_row, k_row = gains[0:1, :], gains[1:2, :]
    for a in range(0, width, HD):
        part = slice(a, a + HD)
        query = normed(query_raw[:, part], q_row[:, part])
        key = normed(key_raw[:, part], k_row[:, part])
        queries[:, part] = query[first:]
        keys[:, part] = key
        attended[:, part] = attend(
            starts, query[:first], key, value[:, part], near_keys[:, part], near_values[:, part]
        )


def qkv_kernel(kind, rows_mine, rows_other, w, gains, *refs):
    x, (*queries, keys, values) = refs[:2], refs[2:]
    rows = keys.shape[0]
    width = w.shape[2]
    table = (rows_mine, rows_other)
    low, high = halves_of(kind, x, None, 0, rows)
    moved = modulated(low, high, table_row(table, SHIFT), table_row(table, SCALE))
    query_raw = dot(moved, w[0])
    key_raw = dot(moved, w[1])
    values[...] = dot(moved, w[2]).astype(jnp.bfloat16)
    q_row, k_row = gains[0:1, :], gains[1:2, :]
    for a in range(0, width, HD):
        part = slice(a, a + HD)
        query = normed(query_raw[:, part], q_row[:, part])
        keys[:, part] = normed(key_raw[:, part], k_row[:, part])
        for n, chunk in enumerate(queries):
            chunk[:, part] = query[n * chunk.shape[0] : (n + 1) * chunk.shape[0]]


def rest_kernel(starts, queries, keys, values, near_keys, near_values, attended):
    for a in range(0, attended.shape[1], HD):
        part = slice(a, a + HD)
        attended[:, part] = attend(
            starts, queries[:, part], keys[:, part], values[:, part], near_keys[:, part], near_values[:, part]
        )


def step_size_of(levels):
    position = lax.axis_index("queue")
    level = levels[position]
    below = levels[jnp.maximum(position - 1, 0)]
    t_cur = (level.astype(jnp.float32) + 1.0) / LEVELS
    t_next = jnp.where(position > 0, (below.astype(jnp.float32) + 1.0) / LEVELS, jnp.float32(0.0))
    return t_next - t_cur


def project_kernel(kind, step, row, levels, rows_mine, rows_other, w_mine, w_other, a_mine, a_other, *refs):
    x, new = refs[:-1], refs[-1]
    count = new.shape[0]
    width = new.shape[1] // 2
    gate = table_row((rows_mine, rows_other), GATE)
    halves = halves_of(kind, x, step - 1, row, count)
    product = dot(a_mine[...], w_mine[...]) + dot(a_other[...], w_other[...])
    for n in range(2):
        part = slice(n * width, (n + 1) * width)
        velocity = gate[n] * product[:, part]
        value = (halves[n].astype(jnp.float32) + step_size_of(levels) * velocity).astype(jnp.bfloat16)
        new[:, part] = value


def final_kernel(kind, step, row, levels, rows_mine, w_mine, w_other, a_mine, a_other, *refs):
    x, (new, velocity_out) = refs[:-2], refs[-2:]
    count, width = new.shape
    half = lax.axis_index("heads")
    part = pl.ds(pl.multiple_of(half * width, HD), width)
    low, high = halves_of(kind, x, step - 1, row, count)
    held = jnp.where(half == 0, low, high).astype(jnp.float32)
    product = dot(a_mine[...], w_mine[:, part]) + dot(a_other[...], w_other[:, part])
    velocity = rows_mine[GATE : GATE + 1, :].astype(jnp.float32) * product
    velocity_out[...] = velocity.astype(jnp.bfloat16)
    new[...] = (held + step_size_of(levels) * velocity).astype(jnp.bfloat16)


def piece_of(position):
    core = position % 2
    z = (position // 4) % 8
    y = position // 32
    return (y + 2 * z) % 4, core


def gather_kernel(own, back, ahead, across, others, w_other):
    group, core = piece_of(lax.axis_index("queue"))
    size = own.shape[0]
    for n, (block, turn) in enumerate(((own, 0), (back, 3), (ahead, 1), (across, 2))):
        place = (group + turn) % 4 * 2
        w_other[pl.ds(pl.multiple_of((place + core) * size, 16), size), :] = block[...]
        w_other[pl.ds(pl.multiple_of((place + 1 - core) * size, 16), size), :] = others[n]


def kernel_call(kernel, out, scalars, arrays, products=0, exponentials=0, dtype=jnp.bfloat16):
    many = isinstance(out[0], tuple)
    outs = out if many else (out,)
    shapes = tuple(jax.ShapeDtypeStruct(s, dtype) for s in outs)
    size = sum(a.size * a.dtype.itemsize for a in arrays)
    result = pl.pallas_call(
        kernel,
        cost_estimate=pl.CostEstimate(
            flops=2 * products, bytes_accessed=size, transcendentals=exponentials
        ),
        out_shape=shapes,
        in_specs=[pl.BlockSpec(memory_space=pltpu.SMEM)] * len(scalars)
        + [pl.BlockSpec(memory_space=pltpu.VMEM)] * len(arrays),
        out_specs=tuple([pl.BlockSpec(memory_space=pltpu.VMEM)] * len(outs)),
        compiler_params=pltpu.CompilerParams(vmem_limit_bytes=VMEM_LIMIT),
    )(*scalars, *arrays)
    return result if many else result[0]


def after(block, *others):
    return lax.optimization_barrier((block, *others))[0]


def fetched_piece(w_out):
    size = w_out.shape[0] // 8
    group, core = piece_of(lax.axis_index("queue"))
    return lax.dynamic_slice_in_dim(w_out, (group * 2 + core) * size, size, 0)


def other_projection(own, ready, shape):
    def turned(y, z):
        return lambda q, h: ((q // 32 + y) % 4 * 32 + (q // 4 + z) % 8 * 4 + q % 4, h)

    back = routed(own, turned(1, 0))
    ahead = routed(own, turned(-1, 0))
    across = routed(own, turned(0, 1))
    own, back, ahead, across, _ = lax.optimization_barrier((own, back, ahead, across, ready))
    others = routed(jnp.stack([own, back, ahead, across]), lambda q, h: (q ^ 1, h))
    return kernel_call(gather_kernel, shape, (), (own, back, ahead, across, others))


def on_device(
    frames,
    fresh_groups,
    level_index,
    window_start,
    mod_shift,
    mod_scale,
    mod_gate,
    w_qkv,
    q_gain,
    k_gain,
    w_out,
):
    position = lax.axis_index("queue")
    last = lax.axis_size("queue") - 1
    rows, width = frames.shape
    count = rows // CHUNKS
    w = jnp.transpose(w_qkv, (1, 0, 2))
    group_products = rows * w.shape[1] * width
    attention_products = 4 * count * rows * width
    out_products = 2 * count * width * width

    def swap(block):
        return routed(block, lambda q, h: (q, 1 - h))

    def up(block):
        return routed(block, lambda q, h: (q + 1, h))

    def down(block):
        return routed(block, lambda q, h: (q - 1, h))

    other = swap(frames)
    rows_mine = rows_call(level_index, (mod_shift, mod_scale, mod_gate))
    rows_other = swap(rows_mine)
    w_out_hbm = w_out
    w, gains, fresh, w_out = stage_call(w, q_gain, k_gain, fresh_groups, w_out)
    near_mine = up(frames)
    piece = routed(after(fetched_piece(w_out_hbm), other, rows_other, gains, near_mine), lambda q, h: (q ^ 2, 1 - h))
    near_other = up(after(other, rows_other, gains, near_mine))
    piece = routed(after(fetched_piece(w_out_hbm), other, rows_other, gains, near_mine), lambda q, h: (q ^ 2, 1 - h))
    table = (rows_mine, rows_other)
    kind, state = "pair", (frames, other)
    near_kind, near = "pair", (near_mine, near_other)
    *queries, keys, values = kernel_call(
        functools.partial(qkv_kernel, kind),
        ((count, width),) * CHUNKS + ((rows, width),) * 2,
        (),
        (*table, w, gains, *state),
        3 * group_products,
    )
    near = (near_mine, after(near_other, keys))
    for step in range(STEPS):
        near_keys, near_values = kernel_call(
            functools.partial(near_kernel, near_kind),
            ((rows, width), (rows, width)),
            (),
            (*table, w, gains, *near),
            2 * group_products,
        )
        parts = []
        if step > 0:
            first, *queries, keys, values = kernel_call(
                functools.partial(own_kernel, kind, step - 1, count),
                ((count, width), (rows - count, width), (rows, width), (rows, width)),
                (window_start,),
                (*table, w, gains, near_keys, near_values, *state),
                3 * group_products + attention_products,
                attention_products // HD,
            )
            parts = [first]
        for query in queries:
            rest = kernel_call(
                rest_kernel,
                (count, width),
                (window_start,),
                (after(query, *parts), keys, values, near_keys, near_values),
                attention_products,
                attention_products // HD,
            )
            parts.append(rest)
        received = [swap(part) for part in parts]
        received[0] = after(received[0], parts[1])
        if step == 0:
            w_other = other_projection(piece, received[0], w_out.shape)
        if step < STEPS - 1:
            new = []
            for n in range(CHUNKS):
                block = kernel_call(
                    functools.partial(project_kernel, kind, step, n * count),
                    (count, 2 * width),
                    (level_index,),
                    (*table, w_out, w_other, parts[n], after(received[n], *new), *state),
                    2 * out_products,
                )
                new.append(block)
            if step == 0:
                fresh_other = routed(
                    after(fresh, keys),
                    lambda q, h: (last, 1 - h) if q == last - 2 else None,
                )
            state = (fresh, fresh_other, *[down(block) for block in new])
            near_kind, near = "chunks", (fresh, fresh_other, *(after(block, state[2]) for block in new))
            kind = "fresh"
        else:
            done = []
            for n in range(CHUNKS):
                pair = kernel_call(
                    functools.partial(final_kernel, kind, step, n * count),
                    ((count, width), (count, width)),
                    (level_index,),
                    (rows_mine, w_out, w_other, parts[n], after(received[n], *(p[0] for p in done)), *state),
                    out_products,
                )
                done.append(pair)
            advanced = jnp.concatenate([down(block) for block, _ in done], axis=0)
            velocity = jnp.concatenate([block for _, block in done], axis=0)
            final = jnp.where(position == last, fresh_groups[step], advanced)
    return (final, velocity)


def solution(mesh):
    placed = (
        P("queue", "heads"),
        P(None, None, "heads"),
        P(),
        P(),
        P(None, "heads"),
        P(None, "heads"),
        P(None, "heads"),
        P(None, None, "heads"),
        P("heads"),
        P("heads"),
        P("heads", None),
    )
    return jax.shard_map(
        on_device,
        mesh=mesh,
        in_specs=placed,
        out_specs=(P("queue", "heads"), P("queue", "heads")),
        check_vma=False,
    )
```

```python
import functools

import jax
import jax.numpy as jnp
from jax import lax
from jax.experimental import pallas as pl
from jax.experimental.pallas import tpu as pltpu
from jax.sharding import PartitionSpec as P

HD = 128
STEPS = 3
LEVELS = 64
EPS = 1e-06
AXES = ("queue", "heads")
VMEM_LIMIT = 24 * 1024 * 1024
CHUNKS = 2
SHIFT, SCALE, GATE, NEAR_SHIFT, NEAR_SCALE = range(5)
TABLE_ROWS = 16


def routed(block, target):
    slots, halves = lax.axis_size("queue"), lax.axis_size("heads")
    pairs = []
    for q in range(slots):
        for h in range(halves):
            to = target(q, h)
            if to is not None and 0 <= to[0] < slots:
                pairs.append((q * halves + h, to[0] * halves + to[1]))
    return lax.ppermute(block, AXES, pairs)


def dot(a, b):
    return jnp.dot(a, b, preferred_element_type=jnp.float32)


def dot_t(a, b):
    return lax.dot_general(a, b, (((1,), (1,)), ((), ())), preferred_element_type=jnp.float32)


def modulated(low, high, shift, scale):
    low, high = low.astype(jnp.float32), high.astype(jnp.float32)
    total = jnp.sum(low * low, axis=-1, keepdims=True) + jnp.sum(high * high, axis=-1, keepdims=True)
    factor = lax.rsqrt(total / (2 * low.shape[-1]) + EPS)
    parts = [low, high]
    for n in range(2):
        parts[n] = (parts[n] * factor * (1.0 + scale[n]) + shift[n]).astype(jnp.bfloat16)
    return jnp.concatenate(parts, axis=-1)


def normed(block, gain):
    mean = jnp.mean(block * block, axis=-1, keepdims=True)
    return (block * lax.rsqrt(mean + EPS) * gain).astype(jnp.bfloat16)


def ordered(mine, other):
    first = lax.axis_index("heads") == 0
    return jnp.where(first, mine, other), jnp.where(first, other, mine)


def table_row(rows, n):
    mine, other = (r[n : n + 1, :].astype(jnp.float32) for r in rows)
    return ordered(mine, other)


def halves_of(kind, refs, step, row, count):
    if kind == "pair":
        return ordered(refs[0][row : row + count, :], refs[1][row : row + count, :])
    chunks = refs if kind == "chunks" else refs[2:]
    size = chunks[0].shape[0]
    wide = [c[...] for c in chunks[row // size : (row + count) // size]]
    wide = wide[0] if len(wide) == 1 else jnp.concatenate(wide, axis=0)
    width = wide.shape[1] // 2
    low, high = wide[:, :width], wide[:, width:]
    if kind == "chunks":
        return low, high
    passed = ordered(*(group[row : row + count, :] for group in refs[:2]))
    last = lax.axis_index("queue") == lax.axis_size("queue") - 1
    return jnp.where(last, passed[0], low), jnp.where(last, passed[1], high)


def rows_kernel(levels_hbm, shift_hbm, scale_hbm, gate_hbm, rows, levels, shift, scale, gate, arrived):
    tables = ((levels_hbm, levels), (shift_hbm, shift), (scale_hbm, scale), (gate_hbm, gate))
    copies = [pltpu.make_async_copy(a, b, arrived.at[n]) for n, (a, b) in enumerate(tables)]
    for copy in copies:
        copy.start()
    for copy in copies:
        copy.wait()
    position = lax.axis_index("queue")
    level = levels[position]
    below = levels[jnp.maximum(position - 1, 0)]
    shape = (TABLE_ROWS, shift.shape[0])
    row = lax.broadcasted_iota(jnp.int32, shape, 0)
    column = lax.broadcasted_iota(jnp.int32, shape, 1)

    def picked(table, own, near):
        chosen = jnp.logical_and(row == own, column == level)
        if near is not None:
            chosen = jnp.logical_or(chosen, jnp.logical_and(row == near, column == below))
        return dot(jnp.where(chosen, 1.0, 0.0).astype(jnp.bfloat16), table[...])

    out = picked(shift, SHIFT, NEAR_SHIFT) + picked(scale, SCALE, NEAR_SCALE)
    rows[...] = (out + picked(gate, GATE, None)).astype(jnp.bfloat16)


def rows_call(levels, tables):
    held = [pltpu.VMEM(table.shape, table.dtype) for table in tables]
    return pl.pallas_call(
        rows_kernel,
        out_shape=jax.ShapeDtypeStruct((TABLE_ROWS, tables[0].shape[1]), jnp.bfloat16),
        in_specs=[pl.BlockSpec(memory_space=pl.ANY)] * (1 + len(tables)),
        out_specs=pl.BlockSpec(memory_space=pltpu.VMEM),
        scratch_shapes=[pltpu.SMEM(levels.shape, levels.dtype)] + held + [pltpu.SemaphoreType.DMA((1 + len(tables),))],
        compiler_params=pltpu.CompilerParams(vmem_limit_bytes=VMEM_LIMIT),
    )(*(pltpu.with_memory_space_constraint(a, pltpu.HBM) for a in (levels, *tables)))


def stage_kernel(w_hbm, q_hbm, k_hbm, fresh_hbm, w_out_hbm, w, gains, *refs):
    *fresh, w_out, q_gain, k_gain, arrived = refs
    moves = [(w_hbm, w), (q_hbm, q_gain), (k_hbm, k_gain), (w_out_hbm, w_out)]
    moves += [(fresh_hbm.at[n], group) for n, group in enumerate(fresh)]
    copies = [pltpu.make_async_copy(a, b, arrived.at[n]) for n, (a, b) in enumerate(moves)]
    for copy in copies:
        copy.start()
    for copy in copies:
        copy.wait()
    gains[0:1, :] = q_gain[...].reshape(1, -1)
    gains[1:2, :] = k_gain[...].reshape(1, -1)


def stage_call(w, q_gain, k_gain, fresh, w_out):
    vmem = pl.BlockSpec(memory_space=pltpu.VMEM)
    held = [pltpu.with_memory_space_constraint(a, pltpu.HBM) for a in (w, q_gain, k_gain, fresh, w_out)]
    groups = [pltpu.VMEM(fresh.shape[1:], fresh.dtype)] * STEPS
    return pl.pallas_call(
        stage_kernel,
        out_shape=(
            pltpu.VMEM(w.shape, w.dtype),
            pltpu.VMEM((2, q_gain.shape[0]), q_gain.dtype),
            *groups,
            pltpu.VMEM(w_out.shape, w_out.dtype),
        ),
        in_specs=[pl.BlockSpec(memory_space=pl.ANY)] * 5,
        out_specs=(vmem,) * (3 + len(groups)),
        scratch_shapes=[
            pltpu.VMEM(q_gain.shape, q_gain.dtype),
            pltpu.VMEM(k_gain.shape, k_gain.dtype),
            pltpu.SemaphoreType.DMA((4 + len(groups),)),
        ],
        compiler_params=pltpu.CompilerParams(vmem_limit_bytes=VMEM_LIMIT),
    )(*held)


def near_kernel(kind, rows_mine, rows_other, w, gains, *refs):
    x, (keys, values) = refs[:-2], refs[-2:]
    width = w.shape[2]
    table = (rows_mine, rows_other)
    low, high = halves_of(kind, x, None, 0, keys.shape[0])
    moved = modulated(low, high, table_row(table, NEAR_SHIFT), table_row(table, NEAR_SCALE))
    raw = dot(moved, w[1])
    gain = gains[1:2, :]
    for a in range(0, width, HD):
        keys[:, a : a + HD] = normed(raw[:, a : a + HD], gain[:, a : a + HD])
    values[...] = dot(moved, w[2]).astype(jnp.bfloat16)


def attend(starts, attended, queries, keys, values, near_keys, near_values):
    position = lax.axis_index("queue")
    rows = values.shape[0]
    start = jnp.where(position > 0, starts[position], rows)
    visible = lax.broadcasted_iota(jnp.int32, (1, rows), 1) >= start
    factor = 1.4426950408889634 / (HD**0.5)
    parts = [slice(a, a + HD) for a in range(0, values.shape[1], HD)]
    scores = []
    for n, part in enumerate(parts):
        near = jnp.where(visible, dot_t(queries[n], near_keys[:, part]), jnp.float32(-1e30))
        scores.append((dot_t(queries[n], keys[n]), near))
    tops = [jnp.max(jnp.maximum(own, near), axis=-1, keepdims=True) for own, near in scores]
    weights = [
        (jnp.exp2((own - top) * factor), jnp.exp2((near - top) * factor))
        for (own, near), top in zip(scores, tops)
    ]
    totals = [jnp.sum(own + near, axis=-1, keepdims=True) for own, near in weights]
    for part, (own, near), total in zip(parts, weights, totals):
        out = dot(own.astype(jnp.bfloat16), values[:, part])
        out = out + dot(near.astype(jnp.bfloat16), near_values[:, part])
        attended[:, part] = (out / total).astype(jnp.bfloat16)


def own_kernel(kind, step, count, starts, rows_mine, rows_other, w, gains, near_keys, near_values, *refs):
    x, (attended, queries, keys, values) = refs[:-4], refs[-4:]
    rows = keys.shape[0]
    width = w.shape[2]
    first = attended.shape[0]
    table = (rows_mine, rows_other)
    low, high = halves_of(kind, x, step, 0, rows)
    moved = modulated(low, high, table_row(table, SHIFT), table_row(table, SCALE))
    query_raw = dot(moved, w[0])
    key_raw = dot(moved, w[1])
    value = dot(moved, w[2]).astype(jnp.bfloat16)
    values[...] = value
    q_row, k_row = gains[0:1, :], gains[1:2, :]
    query_heads, key_heads = [], []
    for a in range(0, width, HD):
        part = slice(a, a + HD)
        query = normed(query_raw[:, part], q_row[:, part])
        key = normed(key_raw[:, part], k_row[:, part])
        queries[:, part] = query[first:]
        keys[:, part] = key
        query_heads.append(query[:first])
        key_heads.append(key)
    attend(starts, attended, query_heads, key_heads, value, near_keys, near_values)


def qkv_kernel(kind, rows_mine, rows_other, w, gains, *refs):
    x, (*queries, keys, values) = refs[:2], refs[2:]
    rows = keys.shape[0]
    width = w.shape[2]
    table = (rows_mine, rows_other)
    low, high = halves_of(kind, x, None, 0, rows)
    moved = modulated(low, high, table_row(table, SHIFT), table_row(table, SCALE))
    query_raw = dot(moved, w[0])
    key_raw = dot(moved, w[1])
    values[...] = dot(moved, w[2]).astype(jnp.bfloat16)
    q_row, k_row = gains[0:1, :], gains[1:2, :]
    for a in range(0, width, HD):
        part = slice(a, a + HD)
        query = normed(query_raw[:, part], q_row[:, part])
        keys[:, part] = normed(key_raw[:, part], k_row[:, part])
        for n, chunk in enumerate(queries):
            chunk[:, part] = query[n * chunk.shape[0] : (n + 1) * chunk.shape[0]]


def rest_kernel(starts, queries, keys, values, near_keys, near_values, attended):
    parts = [slice(a, a + HD) for a in range(0, attended.shape[1], HD)]
    query_heads = [queries[:, part] for part in parts]
    key_heads = [keys[:, part] for part in parts]
    attend(starts, attended, query_heads, key_heads, values, near_keys, near_values)


def step_size_of(levels):
    position = lax.axis_index("queue")
    level = levels[position]
    below = levels[jnp.maximum(position - 1, 0)]
    t_cur = (level.astype(jnp.float32) + 1.0) / LEVELS
    t_next = jnp.where(position > 0, (below.astype(jnp.float32) + 1.0) / LEVELS, jnp.float32(0.0))
    return t_next - t_cur


def project_kernel(kind, step, row, levels, rows_mine, rows_other, w_mine, w_other, a_mine, a_other, *refs):
    x, new = refs[:-1], refs[-1]
    count = new.shape[0]
    width = new.shape[1] // 2
    gate = table_row((rows_mine, rows_other), GATE)
    halves = halves_of(kind, x, step - 1, row, count)
    product = dot(a_mine[...], w_mine[...]) + dot(a_other[...], w_other[...])
    for n in range(2):
        part = slice(n * width, (n + 1) * width)
        velocity = gate[n] * product[:, part]
        value = (halves[n].astype(jnp.float32) + step_size_of(levels) * velocity).astype(jnp.bfloat16)
        new[:, part] = value


def final_kernel(kind, step, row, levels, rows_mine, w_mine, w_other, a_mine, a_other, *refs):
    x, (new, velocity_out) = refs[:-2], refs[-2:]
    count, width = new.shape
    half = lax.axis_index("heads")
    part = pl.ds(pl.multiple_of(half * width, HD), width)
    low, high = halves_of(kind, x, step - 1, row, count)
    held = jnp.where(half == 0, low, high).astype(jnp.float32)
    product = dot(a_mine[...], w_mine[:, part]) + dot(a_other[...], w_other[:, part])
    velocity = rows_mine[GATE : GATE + 1, :].astype(jnp.float32) * product
    velocity_out[...] = velocity.astype(jnp.bfloat16)
    new[...] = (held + step_size_of(levels) * velocity).astype(jnp.bfloat16)


def entering(advanced, fresh):
    last = lax.axis_index("queue") == lax.axis_size("queue") - 1
    return jnp.where(last, fresh, advanced)


def enter_kernel(advanced, fresh, out):
    out[...] = entering(advanced[...], fresh[: out.shape[0], :])


def finish_kernel(first, advanced, fresh, velocity_first, velocity_rest, final, velocity):
    count = first.shape[0]
    final[:count, :] = first[...]
    final[count:, :] = entering(advanced[...], fresh[count:, :])
    velocity[:count, :] = velocity_first[...]
    velocity[count:, :] = velocity_rest[...]


def piece_of(position):
    core = position % 2
    z = (position // 4) % 8
    y = position // 32
    return (y + 2 * z) % 4, core


def gather_kernel(own, back, ahead, across, others, w_other):
    group, core = piece_of(lax.axis_index("queue"))
    size = own.shape[0]
    for n, (block, turn) in enumerate(((own, 0), (back, 3), (ahead, 1), (across, 2))):
        place = (group + turn) % 4 * 2
        w_other[pl.ds(pl.multiple_of((place + core) * size, 16), size), :] = block[...]
        w_other[pl.ds(pl.multiple_of((place + 1 - core) * size, 16), size), :] = others[n]


def kernel_call(kernel, out, scalars, arrays, products=0, exponentials=0, dtype=jnp.bfloat16):
    many = isinstance(out[0], tuple)
    outs = out if many else (out,)
    shapes = tuple(jax.ShapeDtypeStruct(s, dtype) for s in outs)
    size = sum(a.size * a.dtype.itemsize for a in arrays)
    result = pl.pallas_call(
        kernel,
        cost_estimate=pl.CostEstimate(
            flops=2 * products, bytes_accessed=size, transcendentals=exponentials
        ),
        out_shape=shapes,
        in_specs=[pl.BlockSpec(memory_space=pltpu.SMEM)] * len(scalars)
        + [pl.BlockSpec(memory_space=pltpu.VMEM)] * len(arrays),
        out_specs=tuple([pl.BlockSpec(memory_space=pltpu.VMEM)] * len(outs)),
        compiler_params=pltpu.CompilerParams(vmem_limit_bytes=VMEM_LIMIT),
    )(*scalars, *arrays)
    return result if many else result[0]


def after(block, *others):
    return lax.optimization_barrier((block, *others))[0]


def fetched_piece(w_out):
    size = w_out.shape[0] // 8
    group, core = piece_of(lax.axis_index("queue"))
    return lax.dynamic_slice_in_dim(w_out, (group * 2 + core) * size, size, 0)


def other_projection(own, ready, shape):
    def turned(y, z):
        return lambda q, h: ((q // 32 + y) % 4 * 32 + (q // 4 + z) % 8 * 4 + q % 4, h)

    back = routed(own, turned(1, 0))
    ahead = routed(own, turned(-1, 0))
    across = routed(own, turned(0, -1))
    own, back, ahead, across, _ = lax.optimization_barrier((own, back, ahead, across, ready))
    others = routed(jnp.stack([own, back, ahead, across]), lambda q, h: (q ^ 1, h))
    return kernel_call(gather_kernel, shape, (), (own, back, ahead, across, others))


def on_device(
    frames,
    fresh_groups,
    level_index,
    window_start,
    mod_shift,
    mod_scale,
    mod_gate,
    w_qkv,
    q_gain,
    k_gain,
    w_out,
):
    last = lax.axis_size("queue") - 1
    rows, width = frames.shape
    count = rows // CHUNKS
    w = jnp.transpose(w_qkv, (1, 0, 2))
    group_products = rows * w.shape[1] * width
    attention_products = 4 * count * rows * width
    out_products = 2 * count * width * width

    def swap(block):
        return routed(block, lambda q, h: (q, 1 - h))

    def up(block):
        return routed(block, lambda q, h: (q + 1, h))

    def down(block):
        return routed(block, lambda q, h: (q - 1, h))

    other = swap(frames)
    rows_mine = rows_call(level_index, (mod_shift, mod_scale, mod_gate))
    rows_other = swap(rows_mine)
    w_out_hbm = w_out
    w, gains, *fresh, w_out = stage_call(w, q_gain, k_gain, fresh_groups, w_out)
    near_mine = up(after(frames, other))
    near_other = up(after(other, rows_other, gains))
    piece = routed(after(fetched_piece(w_out_hbm), rows_mine), lambda q, h: (q ^ 2, 1 - h))
    table = (rows_mine, rows_other)
    kind, state = "pair", (frames, other)
    near_kind, near = "pair", (near_mine, near_other)
    *queries, keys, values = kernel_call(
        functools.partial(qkv_kernel, kind),
        ((count, width),) * CHUNKS + ((rows, width),) * 2,
        (),
        (*table, w, gains, *state),
        3 * group_products,
    )
    near = (near_mine, after(near_other, keys))
    for step in range(STEPS):
        near_keys, near_values = kernel_call(
            functools.partial(near_kernel, near_kind),
            ((rows, width), (rows, width)),
            (),
            (*table, w, gains, *near),
            2 * group_products,
        )
        if step < STEPS - 1:
            fresh_other = routed(
                after(fresh[step], near_keys), lambda q, h: (last, 1 - h) if q == last - 2 else None
            )
        parts = []
        if step > 0:
            first, *queries, keys, values = kernel_call(
                functools.partial(own_kernel, kind, step - 1, count),
                ((count, width), (rows - count, width), (rows, width), (rows, width)),
                (window_start,),
                (*table, w, gains, near_keys, near_values, *state),
                3 * group_products + attention_products,
                attention_products // HD,
            )
            parts = [first]
        for query in queries:
            rest = kernel_call(
                rest_kernel,
                (count, width),
                (window_start,),
                (after(query, *parts), keys, values, near_keys, near_values),
                attention_products,
                attention_products // HD,
            )
            parts.append(rest)
        received = [swap(part) for part in parts]
        received[0] = after(received[0], parts[1])
        if step == 0:
            w_other = other_projection(piece, received[0], w_out.shape)
        if step < STEPS - 1:
            new = []
            for n in range(CHUNKS):
                block = kernel_call(
                    functools.partial(project_kernel, kind, step, n * count),
                    (count, 2 * width),
                    (level_index,),
                    (*table, w_out, w_other, parts[n], after(received[n], *new), *state),
                    2 * out_products,
                )
                new.append(block)
            state = (fresh[step], fresh_other, *[down(block) for block in new])
            near_kind, near = "chunks", [after(block, state[2]) for block in new]
            kind = "fresh"
        else:
            done = []
            for n in range(CHUNKS):
                pair = kernel_call(
                    functools.partial(final_kernel, kind, step, n * count),
                    ((count, width), (count, width)),
                    (level_index,),
                    (rows_mine, w_out, w_other, parts[n], after(received[n], *(p[0] for p in done)), *state),
                    out_products,
                )
                done.append(pair)
            advanced = [down(block) for block, _ in done]
            first = kernel_call(enter_kernel, (count, width), (), (advanced[0], fresh[step]))
            final, velocity = kernel_call(
                finish_kernel,
                ((rows, width), (rows, width)),
                (),
                (first, after(advanced[1], first), fresh[step], done[0][1], done[1][1]),
            )
    return (final, velocity)


def solution(mesh):
    placed = (
        P("queue", "heads"),
        P(None, None, "heads"),
        P(),
        P(),
        P(None, "heads"),
        P(None, "heads"),
        P(None, "heads"),
        P(None, None, "heads"),
        P("heads"),
        P("heads"),
        P("heads", None),
    )
    return jax.shard_map(
        on_device,
        mesh=mesh,
        in_specs=placed,
        out_specs=(P("queue", "heads"), P("queue", "heads")),
        check_vma=False,
    )
```

```python
import functools

import jax
import jax.numpy as jnp
from jax import lax
from jax.experimental import pallas as pl
from jax.experimental.pallas import tpu as pltpu
from jax.sharding import PartitionSpec as P

HD = 128
STEPS = 3
LEVELS = 64
EPS = 1e-06
AXES = ("queue", "heads")
VMEM_LIMIT = 24 * 1024 * 1024
CHUNKS = 2
SHIFT, SCALE, GATE, NEAR_SHIFT, NEAR_SCALE = range(5)
TABLE_ROWS = 16


def routed(block, target):
    slots, halves = lax.axis_size("queue"), lax.axis_size("heads")
    pairs = []
    for q in range(slots):
        for h in range(halves):
            to = target(q, h)
            if to is not None and 0 <= to[0] < slots:
                pairs.append((q * halves + h, to[0] * halves + to[1]))
    return lax.ppermute(block, AXES, pairs)


def dot(a, b):
    return jnp.dot(a, b, preferred_element_type=jnp.float32)


def dot_t(a, b):
    return lax.dot_general(a, b, (((1,), (1,)), ((), ())), preferred_element_type=jnp.float32)


def modulated(low, high, shift, scale):
    low, high = low.astype(jnp.float32), high.astype(jnp.float32)
    total = jnp.sum(low * low, axis=-1, keepdims=True) + jnp.sum(high * high, axis=-1, keepdims=True)
    factor = lax.rsqrt(total / (2 * low.shape[-1]) + EPS)
    parts = [low, high]
    for n in range(2):
        parts[n] = (parts[n] * factor * (1.0 + scale[n]) + shift[n]).astype(jnp.bfloat16)
    return jnp.concatenate(parts, axis=-1)


def normed(block, gain):
    mean = jnp.mean(block * block, axis=-1, keepdims=True)
    return (block * lax.rsqrt(mean + EPS) * gain).astype(jnp.bfloat16)


def ordered(mine, other):
    first = lax.axis_index("heads") == 0
    return jnp.where(first, mine, other), jnp.where(first, other, mine)


def table_row(rows, n):
    mine, other = (r[n : n + 1, :].astype(jnp.float32) for r in rows)
    return ordered(mine, other)


def halves_of(kind, refs, row, count):
    if kind == "pair":
        return ordered(refs[0][row : row + count, :], refs[1][row : row + count, :])
    chunks = refs if kind == "chunks" else refs[2:]
    size = chunks[0].shape[0]
    wide = [c[...] for c in chunks[row // size : (row + count) // size]]
    wide = wide[0] if len(wide) == 1 else jnp.concatenate(wide, axis=0)
    width = wide.shape[1] // 2
    low, high = wide[:, :width], wide[:, width:]
    if kind == "chunks":
        return low, high
    passed = ordered(*(group[row : row + count, :] for group in refs[:2]))
    last = lax.axis_index("queue") == lax.axis_size("queue") - 1
    return jnp.where(last, passed[0], low), jnp.where(last, passed[1], high)


def rows_kernel(levels_hbm, shift_hbm, scale_hbm, gate_hbm, rows, levels, shift, scale, gate, arrived):
    tables = ((levels_hbm, levels), (shift_hbm, shift), (scale_hbm, scale), (gate_hbm, gate))
    copies = [pltpu.make_async_copy(a, b, arrived.at[n]) for n, (a, b) in enumerate(tables)]
    for copy in copies:
        copy.start()
    for copy in copies:
        copy.wait()
    position = lax.axis_index("queue")
    level = levels[position]
    below = levels[jnp.maximum(position - 1, 0)]
    shape = (TABLE_ROWS, shift.shape[0])
    row = lax.broadcasted_iota(jnp.int32, shape, 0)
    column = lax.broadcasted_iota(jnp.int32, shape, 1)

    def picked(table, own, near):
        chosen = jnp.logical_and(row == own, column == level)
        if near is not None:
            chosen = jnp.logical_or(chosen, jnp.logical_and(row == near, column == below))
        return dot(jnp.where(chosen, 1.0, 0.0).astype(jnp.bfloat16), table[...])

    out = picked(shift, SHIFT, NEAR_SHIFT) + picked(scale, SCALE, NEAR_SCALE)
    rows[...] = (out + picked(gate, GATE, None)).astype(jnp.bfloat16)


def rows_call(levels, tables):
    held = [pltpu.VMEM(table.shape, table.dtype) for table in tables]
    return pl.pallas_call(
        rows_kernel,
        out_shape=jax.ShapeDtypeStruct((TABLE_ROWS, tables[0].shape[1]), jnp.bfloat16),
        in_specs=[pl.BlockSpec(memory_space=pl.ANY)] * (1 + len(tables)),
        out_specs=pl.BlockSpec(memory_space=pltpu.VMEM),
        scratch_shapes=[pltpu.SMEM(levels.shape, levels.dtype)] + held + [pltpu.SemaphoreType.DMA((1 + len(tables),))],
        compiler_params=pltpu.CompilerParams(vmem_limit_bytes=VMEM_LIMIT),
    )(*(pltpu.with_memory_space_constraint(a, pltpu.HBM) for a in (levels, *tables)))


def stage_kernel(w_hbm, q_hbm, k_hbm, fresh_hbm, w_out_hbm, w, gains, *refs):
    *fresh, w_out, q_gain, k_gain, arrived = refs
    moves = [(w_hbm, w), (q_hbm, q_gain), (k_hbm, k_gain), (w_out_hbm, w_out)]
    moves += [(fresh_hbm.at[n], group) for n, group in enumerate(fresh)]
    copies = [pltpu.make_async_copy(a, b, arrived.at[n]) for n, (a, b) in enumerate(moves)]
    for copy in copies:
        copy.start()
    for copy in copies:
        copy.wait()
    gains[0:1, :] = q_gain[...].reshape(1, -1)
    gains[1:2, :] = k_gain[...].reshape(1, -1)


def stage_call(w, q_gain, k_gain, fresh, w_out):
    vmem = pl.BlockSpec(memory_space=pltpu.VMEM)
    held = [pltpu.with_memory_space_constraint(a, pltpu.HBM) for a in (w, q_gain, k_gain, fresh, w_out)]
    groups = [pltpu.VMEM(fresh.shape[1:], fresh.dtype)] * STEPS
    return pl.pallas_call(
        stage_kernel,
        out_shape=(
            pltpu.VMEM(w.shape, w.dtype),
            pltpu.VMEM((2, q_gain.shape[0]), q_gain.dtype),
            *groups,
            pltpu.VMEM(w_out.shape, w_out.dtype),
        ),
        in_specs=[pl.BlockSpec(memory_space=pl.ANY)] * 5,
        out_specs=(vmem,) * (3 + len(groups)),
        scratch_shapes=[
            pltpu.VMEM(q_gain.shape, q_gain.dtype),
            pltpu.VMEM(k_gain.shape, k_gain.dtype),
            pltpu.SemaphoreType.DMA((4 + len(groups),)),
        ],
        compiler_params=pltpu.CompilerParams(vmem_limit_bytes=VMEM_LIMIT),
    )(*held)


def near_kernel(kind, rows_mine, rows_other, w, gains, *refs):
    x, (keys, values) = refs[:-2], refs[-2:]
    width = w.shape[2]
    table = (rows_mine, rows_other)
    low, high = halves_of(kind, x, 0, keys.shape[0])
    moved = modulated(low, high, table_row(table, NEAR_SHIFT), table_row(table, NEAR_SCALE))
    raw = dot(moved, w[1])
    gain = gains[1:2, :]
    for a in range(0, width, HD):
        keys[:, a : a + HD] = normed(raw[:, a : a + HD], gain[:, a : a + HD])
    values[...] = dot(moved, w[2]).astype(jnp.bfloat16)


def attend(starts, attended, queries, keys, values, near_keys, near_values):
    position = lax.axis_index("queue")
    rows = values.shape[0]
    start = jnp.where(position > 0, starts[position], rows)
    visible = lax.broadcasted_iota(jnp.int32, (1, rows), 1) >= start
    factor = 1.4426950408889634 / (HD**0.5)
    parts = [slice(a, a + HD) for a in range(0, values.shape[1], HD)]
    scores = []
    for n, part in enumerate(parts):
        near = jnp.where(visible, dot_t(queries[n], near_keys[:, part]), jnp.float32(-1e30))
        scores.append((dot_t(queries[n], keys[n]), near))
    tops = [jnp.max(jnp.maximum(own, near), axis=-1, keepdims=True) for own, near in scores]
    weights = [
        (jnp.exp2((own - top) * factor), jnp.exp2((near - top) * factor))
        for (own, near), top in zip(scores, tops)
    ]
    totals = [jnp.sum(own + near, axis=-1, keepdims=True) for own, near in weights]
    for part, (own, near), total in zip(parts, weights, totals):
        out = dot(own.astype(jnp.bfloat16), values[:, part])
        out = out + dot(near.astype(jnp.bfloat16), near_values[:, part])
        attended[:, part] = (out / total).astype(jnp.bfloat16)


def projected(low, high, table, w, gains):
    width = w.shape[2]
    moved = modulated(low, high, table_row(table, SHIFT), table_row(table, SCALE))
    query_raw = dot(moved, w[0])
    key_raw = dot(moved, w[1])
    values = dot(moved, w[2]).astype(jnp.bfloat16)
    parts = [slice(a, a + HD) for a in range(0, width, HD)]
    queries = [normed(query_raw[:, part], gains[0:1, part]) for part in parts]
    keys = [normed(key_raw[:, part], gains[1:2, part]) for part in parts]
    return queries, keys, values


def head_kernel(rows_mine, rows_other, w, gains, fresh, fresh_other, chunk, queries, keys, values):
    low, high = halves_of("fresh", (fresh, fresh_other, chunk), 0, chunk.shape[0])
    heads, key_heads, value = projected(low, high, (rows_mine, rows_other), w, gains)
    values[...] = value
    for n in range(len(heads)):
        queries[:, n * HD : (n + 1) * HD] = heads[n]
        keys[:, n * HD : (n + 1) * HD] = key_heads[n]


def own_kernel(
    starts, rows_mine, rows_other, w, gains, near_keys, near_values, first_queries, first_keys, first_values,
    fresh, fresh_other, first, rest, attended, queries, keys, values,
):
    count = rest.shape[0]
    low, high = halves_of("fresh", (fresh, fresh_other, first, rest), count, count)
    heads, key_heads, value = projected(low, high, (rows_mine, rows_other), w, gains)
    values[:count, :] = first_values[...]
    values[count:, :] = value
    keys[:count, :] = first_keys[...]
    first_heads, all_keys = [], []
    for n in range(len(heads)):
        part = slice(n * HD, (n + 1) * HD)
        queries[:, part] = heads[n]
        keys[count:, part] = key_heads[n]
        first_heads.append(first_queries[:, part])
        all_keys.append(keys[:, part])
    attend(starts, attended, first_heads, all_keys, values, near_keys, near_values)


def qkv_kernel(rows_mine, rows_other, w, gains, mine, other, *refs):
    *queries, keys, values = refs
    low, high = halves_of("pair", (mine, other), 0, keys.shape[0])
    heads, key_heads, value = projected(low, high, (rows_mine, rows_other), w, gains)
    values[...] = value
    for n in range(len(heads)):
        part = slice(n * HD, (n + 1) * HD)
        keys[:, part] = key_heads[n]
        for c, chunk in enumerate(queries):
            chunk[:, part] = heads[n][c * chunk.shape[0] : (c + 1) * chunk.shape[0]]


def rest_kernel(starts, queries, keys, values, near_keys, near_values, attended):
    parts = [slice(a, a + HD) for a in range(0, attended.shape[1], HD)]
    query_heads = [queries[:, part] for part in parts]
    key_heads = [keys[:, part] for part in parts]
    attend(starts, attended, query_heads, key_heads, values, near_keys, near_values)


def step_size_of(levels):
    position = lax.axis_index("queue")
    level = levels[position]
    below = levels[jnp.maximum(position - 1, 0)]
    t_cur = (level.astype(jnp.float32) + 1.0) / LEVELS
    t_next = jnp.where(position > 0, (below.astype(jnp.float32) + 1.0) / LEVELS, jnp.float32(0.0))
    return t_next - t_cur


def project_kernel(kind, row, levels, rows_mine, rows_other, w_mine, w_other, a_mine, a_other, *refs):
    x, new = refs[:-1], refs[-1]
    count = new.shape[0]
    width = new.shape[1] // 2
    gate = table_row((rows_mine, rows_other), GATE)
    halves = halves_of(kind, x, row, count)
    product = dot(a_mine[...], w_mine[...]) + dot(a_other[...], w_other[...])
    for n in range(2):
        part = slice(n * width, (n + 1) * width)
        velocity = gate[n] * product[:, part]
        value = (halves[n].astype(jnp.float32) + step_size_of(levels) * velocity).astype(jnp.bfloat16)
        new[:, part] = value


def final_kernel(kind, row, levels, rows_mine, w_mine, w_other, a_mine, a_other, *refs):
    x, (new, velocity_out) = refs[:-2], refs[-2:]
    count, width = new.shape
    half = lax.axis_index("heads")
    part = pl.ds(pl.multiple_of(half * width, HD), width)
    low, high = halves_of(kind, x, row, count)
    held = jnp.where(half == 0, low, high).astype(jnp.float32)
    product = dot(a_mine[...], w_mine[:, part]) + dot(a_other[...], w_other[:, part])
    velocity = rows_mine[GATE : GATE + 1, :].astype(jnp.float32) * product
    velocity_out[...] = velocity.astype(jnp.bfloat16)
    new[...] = (held + step_size_of(levels) * velocity).astype(jnp.bfloat16)


def entering(advanced, fresh):
    last = lax.axis_index("queue") == lax.axis_size("queue") - 1
    return jnp.where(last, fresh, advanced)


def enter_kernel(advanced, fresh, out):
    out[...] = entering(advanced[...], fresh[: out.shape[0], :])


def finish_kernel(first, advanced, fresh, velocity_first, velocity_rest, final, velocity):
    count = first.shape[0]
    final[:count, :] = first[...]
    final[count:, :] = entering(advanced[...], fresh[count:, :])
    velocity[:count, :] = velocity_first[...]
    velocity[count:, :] = velocity_rest[...]


def piece_of(position):
    core = position % 2
    z = (position // 4) % 8
    y = position // 32
    return (y + 2 * z) % 4, core


def gather_kernel(own, back, ahead, across, others, w_other):
    group, core = piece_of(lax.axis_index("queue"))
    size = own.shape[0]
    for n, (block, turn) in enumerate(((own, 0), (back, 3), (ahead, 1), (across, 2))):
        place = (group + turn) % 4 * 2
        w_other[pl.ds(pl.multiple_of((place + core) * size, 16), size), :] = block[...]
        w_other[pl.ds(pl.multiple_of((place + 1 - core) * size, 16), size), :] = others[n]


def kernel_call(kernel, out, scalars, arrays, products=0, exponentials=0, dtype=jnp.bfloat16):
    many = isinstance(out[0], tuple)
    outs = out if many else (out,)
    shapes = tuple(jax.ShapeDtypeStruct(s, dtype) for s in outs)
    size = sum(a.size * a.dtype.itemsize for a in arrays)
    result = pl.pallas_call(
        kernel,
        cost_estimate=pl.CostEstimate(
            flops=2 * products, bytes_accessed=size, transcendentals=exponentials
        ),
        out_shape=shapes,
        in_specs=[pl.BlockSpec(memory_space=pltpu.SMEM)] * len(scalars)
        + [pl.BlockSpec(memory_space=pltpu.VMEM)] * len(arrays),
        out_specs=tuple([pl.BlockSpec(memory_space=pltpu.VMEM)] * len(outs)),
        compiler_params=pltpu.CompilerParams(vmem_limit_bytes=VMEM_LIMIT),
    )(*scalars, *arrays)
    return result if many else result[0]


def after(block, *others):
    return lax.optimization_barrier((block, *others))[0]


def fetched_piece(w_out):
    size = w_out.shape[0] // 8
    group, core = piece_of(lax.axis_index("queue"))
    return lax.dynamic_slice_in_dim(w_out, (group * 2 + core) * size, size, 0)


def other_projection(own, ready, shape):
    def turned(y, z):
        return lambda q, h: ((q // 32 + y) % 4 * 32 + (q // 4 + z) % 8 * 4 + q % 4, h)

    back = routed(own, turned(1, 0))
    ahead = routed(own, turned(-1, 0))
    across = routed(own, turned(0, -1))
    own, back, ahead, across, _ = lax.optimization_barrier((own, back, ahead, across, ready))
    others = routed(jnp.stack([own, back, ahead, across]), lambda q, h: (q ^ 1, h))
    return kernel_call(gather_kernel, shape, (), (own, back, ahead, across, others))


def on_device(
    frames,
    fresh_groups,
    level_index,
    window_start,
    mod_shift,
    mod_scale,
    mod_gate,
    w_qkv,
    q_gain,
    k_gain,
    w_out,
):
    last = lax.axis_size("queue") - 1
    rows, width = frames.shape
    count = rows // CHUNKS
    w = jnp.transpose(w_qkv, (1, 0, 2))
    group_products = rows * w.shape[1] * width
    attention_products = 4 * count * rows * width
    out_products = 2 * count * width * width

    def swap(block):
        return routed(block, lambda q, h: (q, 1 - h))

    def up(block):
        return routed(block, lambda q, h: (q + 1, h))

    def down(block):
        return routed(block, lambda q, h: (q - 1, h))

    other = swap(frames)
    rows_mine = rows_call(level_index, (mod_shift, mod_scale, mod_gate))
    rows_other = swap(rows_mine)
    w_out_hbm = w_out
    w, gains, *fresh, w_out = stage_call(w, q_gain, k_gain, fresh_groups, w_out)
    near_mine = up(after(frames, other))
    near_other = up(after(other, rows_other, gains))
    piece = routed(after(fetched_piece(w_out_hbm), rows_mine), lambda q, h: (q ^ 2, 1 - h))
    table = (rows_mine, rows_other)
    kind, state = "pair", (frames, other)
    near_kind, near = "pair", (near_mine, near_other)
    *queries, keys, values = kernel_call(
        qkv_kernel,
        ((count, width),) * CHUNKS + ((rows, width),) * 2,
        (),
        (*table, w, gains, *state),
        3 * group_products,
    )
    near = (near_mine, after(near_other, keys))
    for step in range(STEPS):
        near_keys, near_values = kernel_call(
            functools.partial(near_kernel, near_kind),
            ((rows, width), (rows, width)),
            (),
            (*table, w, gains, *near),
            2 * group_products,
        )
        parts = []
        if step > 0:
            head = kernel_call(
                head_kernel,
                ((count, width),) * 3,
                (),
                (*table, w, gains, *state[:3]),
            )
            first, *queries, keys, values = kernel_call(
                own_kernel,
                ((count, width), (rows - count, width), (rows, width), (rows, width)),
                (window_start,),
                (*table, w, gains, near_keys, near_values, *head, *state),
                3 * group_products + attention_products,
                attention_products // HD,
            )
            parts = [first]
        for query in queries:
            rest = kernel_call(
                rest_kernel,
                (count, width),
                (window_start,),
                (after(query, *parts), keys, values, near_keys, near_values),
                attention_products,
                attention_products // HD,
            )
            parts.append(rest)
        received = [swap(part) for part in parts]
        waits = []
        if step < STEPS - 1:
            fresh_other = routed(
                after(fresh[step], near_keys), lambda q, h: (last, 1 - h) if q == last - 2 else None
            )
            waits = [fresh_other]
        received[0] = after(received[0], parts[1], *waits)
        if step == 0:
            w_other = other_projection(piece, parts[1], w_out.shape)
        if step < STEPS - 1:
            new = []
            for n in range(CHUNKS):
                block = kernel_call(
                    functools.partial(project_kernel, kind, n * count),
                    (count, 2 * width),
                    (level_index,),
                    (*table, w_out, w_other, parts[n], after(received[n], *new), *state),
                    2 * out_products,
                )
                new.append(block)
            state = (fresh[step], fresh_other, *[down(block) for block in new])
            near_kind, near = "chunks", [after(block, state[2]) for block in new]
            kind = "fresh"
        else:
            done = []
            for n in range(CHUNKS):
                pair = kernel_call(
                    functools.partial(final_kernel, kind, n * count),
                    ((count, width), (count, width)),
                    (level_index,),
                    (rows_mine, w_out, w_other, parts[n], after(received[n], *(p[0] for p in done)), *state),
                    out_products,
                )
                done.append(pair)
            advanced = [down(block) for block, _ in done]
            first = kernel_call(enter_kernel, (count, width), (), (advanced[0], fresh[step]))
            final, velocity = kernel_call(
                finish_kernel,
                ((rows, width), (rows, width)),
                (),
                (first, after(advanced[1], first), fresh[step], done[0][1], done[1][1]),
            )
    return (final, velocity)


def solution(mesh):
    placed = (
        P("queue", "heads"),
        P(None, None, "heads"),
        P(),
        P(),
        P(None, "heads"),
        P(None, "heads"),
        P(None, "heads"),
        P(None, None, "heads"),
        P("heads"),
        P("heads"),
        P("heads", None),
    )
    return jax.shard_map(
        on_device,
        mesh=mesh,
        in_specs=placed,
        out_specs=(P("queue", "heads"), P("queue", "heads")),
        check_vma=False,
    )
```

```python
import functools

import jax
import jax.numpy as jnp
from jax import lax
from jax.experimental import pallas as pl
from jax.experimental.pallas import tpu as pltpu
from jax.sharding import PartitionSpec as P

HD = 128
STEPS = 3
LEVELS = 64
EPS = 1e-06
AXES = ("queue", "heads")
VMEM_LIMIT = 24 * 1024 * 1024
CHUNKS = 2
SHIFT, SCALE, GATE, NEAR_SHIFT, NEAR_SCALE = range(5)
TABLE_ROWS = 16


def routed(block, target):
    slots, halves = lax.axis_size("queue"), lax.axis_size("heads")
    pairs = []
    for q in range(slots):
        for h in range(halves):
            to = target(q, h)
            if to is not None and 0 <= to[0] < slots:
                pairs.append((q * halves + h, to[0] * halves + to[1]))
    return lax.ppermute(block, AXES, pairs)


def dot(a, b):
    return jnp.dot(a, b, preferred_element_type=jnp.float32)


def dot_t(a, b):
    return lax.dot_general(a, b, (((1,), (1,)), ((), ())), preferred_element_type=jnp.float32)


def modulated(low, high, shift, scale):
    low, high = low.astype(jnp.float32), high.astype(jnp.float32)
    total = jnp.sum(low * low, axis=-1, keepdims=True) + jnp.sum(high * high, axis=-1, keepdims=True)
    factor = lax.rsqrt(total / (2 * low.shape[-1]) + EPS)
    parts = [low, high]
    for n in range(2):
        parts[n] = (parts[n] * factor * (1.0 + scale[n]) + shift[n]).astype(jnp.bfloat16)
    return jnp.concatenate(parts, axis=-1)


def normed(block, gain):
    mean = jnp.mean(block * block, axis=-1, keepdims=True)
    return (block * lax.rsqrt(mean + EPS) * gain).astype(jnp.bfloat16)


def ordered(mine, other):
    first = lax.axis_index("heads") == 0
    return jnp.where(first, mine, other), jnp.where(first, other, mine)


def table_row(rows, n):
    mine, other = (r[n : n + 1, :].astype(jnp.float32) for r in rows)
    return ordered(mine, other)


def halves_of(kind, refs, row, count):
    if kind == "pair":
        return ordered(refs[0][row : row + count, :], refs[1][row : row + count, :])
    chunks = refs if kind == "chunks" else refs[2:]
    size = chunks[0].shape[0]
    wide = [c[...] for c in chunks[row // size : (row + count) // size]]
    wide = wide[0] if len(wide) == 1 else jnp.concatenate(wide, axis=0)
    width = wide.shape[1] // 2
    low, high = wide[:, :width], wide[:, width:]
    if kind == "chunks":
        return low, high
    passed = ordered(*(group[row : row + count, :] for group in refs[:2]))
    last = lax.axis_index("queue") == lax.axis_size("queue") - 1
    return jnp.where(last, passed[0], low), jnp.where(last, passed[1], high)


def rows_kernel(levels_hbm, shift_hbm, scale_hbm, gate_hbm, rows, levels, shift, scale, gate, arrived):
    tables = ((levels_hbm, levels), (shift_hbm, shift), (scale_hbm, scale), (gate_hbm, gate))
    copies = [pltpu.make_async_copy(a, b, arrived.at[n]) for n, (a, b) in enumerate(tables)]
    for copy in copies:
        copy.start()
    for copy in copies:
        copy.wait()
    position = lax.axis_index("queue")
    level = levels[position]
    below = levels[jnp.maximum(position - 1, 0)]
    shape = (TABLE_ROWS, shift.shape[0])
    row = lax.broadcasted_iota(jnp.int32, shape, 0)
    column = lax.broadcasted_iota(jnp.int32, shape, 1)

    def picked(table, own, near):
        chosen = jnp.logical_and(row == own, column == level)
        if near is not None:
            chosen = jnp.logical_or(chosen, jnp.logical_and(row == near, column == below))
        return dot(jnp.where(chosen, 1.0, 0.0).astype(jnp.bfloat16), table[...])

    out = picked(shift, SHIFT, NEAR_SHIFT) + picked(scale, SCALE, NEAR_SCALE)
    rows[...] = (out + picked(gate, GATE, None)).astype(jnp.bfloat16)


def rows_call(levels, tables):
    held = [pltpu.VMEM(table.shape, table.dtype) for table in tables]
    return pl.pallas_call(
        rows_kernel,
        out_shape=jax.ShapeDtypeStruct((TABLE_ROWS, tables[0].shape[1]), jnp.bfloat16),
        in_specs=[pl.BlockSpec(memory_space=pl.ANY)] * (1 + len(tables)),
        out_specs=pl.BlockSpec(memory_space=pltpu.VMEM),
        scratch_shapes=[pltpu.SMEM(levels.shape, levels.dtype)] + held + [pltpu.SemaphoreType.DMA((1 + len(tables),))],
        compiler_params=pltpu.CompilerParams(vmem_limit_bytes=VMEM_LIMIT),
    )(*(pltpu.with_memory_space_constraint(a, pltpu.HBM) for a in (levels, *tables)))


def stage_kernel(w_hbm, q_hbm, k_hbm, fresh_hbm, w_out_hbm, w, gains, *refs):
    *fresh, w_out, q_gain, k_gain, arrived = refs
    moves = [(w_hbm, w), (q_hbm, q_gain), (k_hbm, k_gain), (w_out_hbm, w_out)]
    moves += [(fresh_hbm.at[n], group) for n, group in enumerate(fresh)]
    copies = [pltpu.make_async_copy(a, b, arrived.at[n]) for n, (a, b) in enumerate(moves)]
    for copy in copies:
        copy.start()
    for copy in copies:
        copy.wait()
    gains[0:1, :] = q_gain[...].reshape(1, -1)
    gains[1:2, :] = k_gain[...].reshape(1, -1)


def stage_call(w, q_gain, k_gain, fresh, w_out):
    vmem = pl.BlockSpec(memory_space=pltpu.VMEM)
    held = [pltpu.with_memory_space_constraint(a, pltpu.HBM) for a in (w, q_gain, k_gain, fresh, w_out)]
    groups = [pltpu.VMEM(fresh.shape[1:], fresh.dtype)] * STEPS
    return pl.pallas_call(
        stage_kernel,
        out_shape=(
            pltpu.VMEM(w.shape, w.dtype),
            pltpu.VMEM((2, q_gain.shape[0]), q_gain.dtype),
            *groups,
            pltpu.VMEM(w_out.shape, w_out.dtype),
        ),
        in_specs=[pl.BlockSpec(memory_space=pl.ANY)] * 5,
        out_specs=(vmem,) * (3 + len(groups)),
        scratch_shapes=[
            pltpu.VMEM(q_gain.shape, q_gain.dtype),
            pltpu.VMEM(k_gain.shape, k_gain.dtype),
            pltpu.SemaphoreType.DMA((4 + len(groups),)),
        ],
        compiler_params=pltpu.CompilerParams(vmem_limit_bytes=VMEM_LIMIT),
    )(*held)


def near_kernel(kind, rows_mine, rows_other, w, gains, *refs):
    x, (keys, values) = refs[:-2], refs[-2:]
    width = w.shape[2]
    table = (rows_mine, rows_other)
    low, high = halves_of(kind, x, 0, keys.shape[0])
    moved = modulated(low, high, table_row(table, NEAR_SHIFT), table_row(table, NEAR_SCALE))
    raw = dot(moved, w[1])
    gain = gains[1:2, :]
    for a in range(0, width, HD):
        keys[:, a : a + HD] = normed(raw[:, a : a + HD], gain[:, a : a + HD])
    values[...] = dot(moved, w[2]).astype(jnp.bfloat16)


def attend(starts, attended, queries, keys, values, near_keys, near_values):
    position = lax.axis_index("queue")
    rows = values.shape[0]
    start = jnp.where(position > 0, starts[position], rows)
    visible = lax.broadcasted_iota(jnp.int32, (1, rows), 1) >= start
    factor = 1.4426950408889634 / (HD**0.5)
    parts = [slice(a, a + HD) for a in range(0, values.shape[1], HD)]
    scores = []
    for n, part in enumerate(parts):
        near = jnp.where(visible, dot_t(queries[n], near_keys[:, part]), jnp.float32(-1e30))
        scores.append((dot_t(queries[n], keys[n]), near))
    tops = [jnp.max(jnp.maximum(own, near), axis=-1, keepdims=True) for own, near in scores]
    weights = [
        (jnp.exp2((own - top) * factor), jnp.exp2((near - top) * factor))
        for (own, near), top in zip(scores, tops)
    ]
    totals = [jnp.sum(own + near, axis=-1, keepdims=True) for own, near in weights]
    for part, (own, near), total in zip(parts, weights, totals):
        out = dot(own.astype(jnp.bfloat16), values[:, part])
        out = out + dot(near.astype(jnp.bfloat16), near_values[:, part])
        attended[:, part] = (out / total).astype(jnp.bfloat16)


def projected(low, high, table, w, gains):
    width = w.shape[2]
    moved = modulated(low, high, table_row(table, SHIFT), table_row(table, SCALE))
    query_raw = dot(moved, w[0])
    key_raw = dot(moved, w[1])
    values = dot(moved, w[2]).astype(jnp.bfloat16)
    parts = [slice(a, a + HD) for a in range(0, width, HD)]
    queries = [normed(query_raw[:, part], gains[0:1, part]) for part in parts]
    keys = [normed(key_raw[:, part], gains[1:2, part]) for part in parts]
    return queries, keys, values


def head_kernel(rows_mine, rows_other, w, gains, fresh, fresh_other, chunk, queries, keys, values):
    low, high = halves_of("fresh", (fresh, fresh_other, chunk), 0, chunk.shape[0])
    heads, key_heads, value = projected(low, high, (rows_mine, rows_other), w, gains)
    values[...] = value
    for n in range(len(heads)):
        queries[:, n * HD : (n + 1) * HD] = heads[n]
        keys[:, n * HD : (n + 1) * HD] = key_heads[n]


def own_kernel(
    starts, rows_mine, rows_other, w, gains, near_keys, near_values, first_queries, first_keys, first_values,
    fresh, fresh_other, first, rest, attended, queries, keys, values,
):
    count = rest.shape[0]
    low, high = halves_of("fresh", (fresh, fresh_other, first, rest), count, count)
    heads, key_heads, value = projected(low, high, (rows_mine, rows_other), w, gains)
    values[:count, :] = first_values[...]
    values[count:, :] = value
    keys[:count, :] = first_keys[...]
    first_heads, all_keys = [], []
    for n in range(len(heads)):
        part = slice(n * HD, (n + 1) * HD)
        queries[:, part] = heads[n]
        keys[count:, part] = key_heads[n]
        first_heads.append(first_queries[:, part])
        all_keys.append(keys[:, part])
    attend(starts, attended, first_heads, all_keys, values, near_keys, near_values)


def qkv_kernel(rows_mine, rows_other, w, gains, mine, other, *refs):
    *queries, keys, values = refs
    low, high = halves_of("pair", (mine, other), 0, keys.shape[0])
    heads, key_heads, value = projected(low, high, (rows_mine, rows_other), w, gains)
    values[...] = value
    for n in range(len(heads)):
        part = slice(n * HD, (n + 1) * HD)
        keys[:, part] = key_heads[n]
        for c, chunk in enumerate(queries):
            chunk[:, part] = heads[n][c * chunk.shape[0] : (c + 1) * chunk.shape[0]]


def rest_kernel(starts, queries, keys, values, near_keys, near_values, attended):
    parts = [slice(a, a + HD) for a in range(0, attended.shape[1], HD)]
    query_heads = [queries[:, part] for part in parts]
    key_heads = [keys[:, part] for part in parts]
    attend(starts, attended, query_heads, key_heads, values, near_keys, near_values)


def step_size_of(levels):
    position = lax.axis_index("queue")
    level = levels[position]
    below = levels[jnp.maximum(position - 1, 0)]
    t_cur = (level.astype(jnp.float32) + 1.0) / LEVELS
    t_next = jnp.where(position > 0, (below.astype(jnp.float32) + 1.0) / LEVELS, jnp.float32(0.0))
    return t_next - t_cur


def mine_kernel(kind, levels, rows_mine, rows_other, w_mine, *refs):
    x, chunks, bases = refs[: -2 * CHUNKS], refs[-2 * CHUNKS : -CHUNKS], refs[-CHUNKS:]
    gate = table_row((rows_mine, rows_other), GATE)
    size = step_size_of(levels)
    for c, (chunk, base) in enumerate(zip(chunks, bases)):
        count, width = chunk.shape[0], base.shape[1] // 2
        halves = halves_of(kind, x, c * count, count)
        product = dot(chunk[...], w_mine[...])
        for n in range(2):
            part = slice(n * width, (n + 1) * width)
            base[:, part] = halves[n].astype(jnp.float32) + size * gate[n] * product[:, part]


def project_kernel(levels, rows_mine, rows_other, w_other, base, a_other, new):
    width = new.shape[1] // 2
    gate = table_row((rows_mine, rows_other), GATE)
    size = step_size_of(levels)
    product = dot(a_other[...], w_other[...])
    for n in range(2):
        part = slice(n * width, (n + 1) * width)
        new[:, part] = (base[:, part] + size * gate[n] * product[:, part]).astype(jnp.bfloat16)


def own_features(width):
    return pl.ds(pl.multiple_of(lax.axis_index("heads") * width, HD), width)


def last_mine_kernel(rows_mine, w_mine, *refs):
    gate = rows_mine[GATE : GATE + 1, :].astype(jnp.float32)
    for chunk, base in zip(refs[:CHUNKS], refs[CHUNKS:]):
        base[...] = gate * dot(chunk[...], w_mine[:, own_features(base.shape[1])])


def final_kernel(kind, row, levels, rows_mine, w_other, base, a_other, *refs):
    x, (new, velocity_out) = refs[:-2], refs[-2:]
    count, width = new.shape
    low, high = halves_of(kind, x, row, count)
    held = jnp.where(lax.axis_index("heads") == 0, low, high).astype(jnp.float32)
    gate = rows_mine[GATE : GATE + 1, :].astype(jnp.float32)
    velocity = base[...] + gate * dot(a_other[...], w_other[:, own_features(width)])
    velocity_out[...] = velocity.astype(jnp.bfloat16)
    new[...] = (held + step_size_of(levels) * velocity).astype(jnp.bfloat16)


def entering(advanced, fresh):
    last = lax.axis_index("queue") == lax.axis_size("queue") - 1
    return jnp.where(last, fresh, advanced)


def enter_kernel(advanced, fresh, out):
    out[...] = entering(advanced[...], fresh[: out.shape[0], :])


def finish_kernel(first, advanced, fresh, velocity_first, velocity_rest, final, velocity):
    count = first.shape[0]
    final[:count, :] = first[...]
    final[count:, :] = entering(advanced[...], fresh[count:, :])
    velocity[:count, :] = velocity_first[...]
    velocity[count:, :] = velocity_rest[...]


def piece_of(position):
    core = position % 2
    z = (position // 4) % 8
    y = position // 32
    return (y + 2 * z) % 4, core


def gather_kernel(own, back, ahead, across, others, w_other):
    group, core = piece_of(lax.axis_index("queue"))
    size = own.shape[0]
    for n, (block, turn) in enumerate(((own, 0), (back, 3), (ahead, 1), (across, 2))):
        place = (group + turn) % 4 * 2
        w_other[pl.ds(pl.multiple_of((place + core) * size, 16), size), :] = block[...]
        w_other[pl.ds(pl.multiple_of((place + 1 - core) * size, 16), size), :] = others[n]


def kernel_call(kernel, out, scalars, arrays, products=0, exponentials=0, dtype=jnp.bfloat16):
    many = isinstance(out[0], tuple)
    outs = out if many else (out,)
    shapes = tuple(jax.ShapeDtypeStruct(s, dtype) for s in outs)
    size = sum(a.size * a.dtype.itemsize for a in arrays)
    result = pl.pallas_call(
        kernel,
        cost_estimate=pl.CostEstimate(
            flops=2 * products, bytes_accessed=size, transcendentals=exponentials
        ),
        out_shape=shapes,
        in_specs=[pl.BlockSpec(memory_space=pltpu.SMEM)] * len(scalars)
        + [pl.BlockSpec(memory_space=pltpu.VMEM)] * len(arrays),
        out_specs=tuple([pl.BlockSpec(memory_space=pltpu.VMEM)] * len(outs)),
        compiler_params=pltpu.CompilerParams(vmem_limit_bytes=VMEM_LIMIT),
    )(*scalars, *arrays)
    return result if many else result[0]


def after(block, *others):
    return lax.optimization_barrier((block, *others))[0]


def fetched_piece(w_out):
    size = w_out.shape[0] // 8
    group, core = piece_of(lax.axis_index("queue"))
    return lax.dynamic_slice_in_dim(w_out, (group * 2 + core) * size, size, 0)


def other_projection(own, ready, shape):
    def turned(y, z):
        return lambda q, h: ((q // 32 + y) % 4 * 32 + (q // 4 + z) % 8 * 4 + q % 4, h)

    back = routed(own, turned(1, 0))
    ahead = routed(own, turned(-1, 0))
    across = routed(own, turned(0, -1))
    own, back, ahead, across, _ = lax.optimization_barrier((own, back, ahead, across, ready))
    others = routed(jnp.stack([own, back, ahead, across]), lambda q, h: (q ^ 1, h))
    return kernel_call(gather_kernel, shape, (), (own, back, ahead, across, others))


def on_device(
    frames,
    fresh_groups,
    level_index,
    window_start,
    mod_shift,
    mod_scale,
    mod_gate,
    w_qkv,
    q_gain,
    k_gain,
    w_out,
):
    last = lax.axis_size("queue") - 1
    rows, width = frames.shape
    count = rows // CHUNKS
    w = jnp.transpose(w_qkv, (1, 0, 2))
    group_products = rows * w.shape[1] * width
    attention_products = 4 * count * rows * width
    out_products = 2 * count * width * width

    def swap(block):
        return routed(block, lambda q, h: (q, 1 - h))

    def up(block):
        return routed(block, lambda q, h: (q + 1, h))

    def down(block):
        return routed(block, lambda q, h: (q - 1, h))

    other = swap(frames)
    rows_mine = rows_call(level_index, (mod_shift, mod_scale, mod_gate))
    rows_other = swap(rows_mine)
    w_out_hbm = w_out
    w, gains, *fresh, w_out = stage_call(w, q_gain, k_gain, fresh_groups, w_out)
    near_mine = up(after(frames, other))
    near_other = up(after(other, rows_other, gains))
    piece = routed(after(fetched_piece(w_out_hbm), rows_mine), lambda q, h: (q ^ 2, 1 - h))
    table = (rows_mine, rows_other)
    kind, state = "pair", (frames, other)
    near_kind, near = "pair", (near_mine, near_other)
    *queries, keys, values = kernel_call(
        qkv_kernel,
        ((count, width),) * CHUNKS + ((rows, width),) * 2,
        (),
        (*table, w, gains, *state),
        3 * group_products,
    )
    near = (near_mine, after(near_other, keys))
    for step in range(STEPS):
        near_keys, near_values = kernel_call(
            functools.partial(near_kernel, near_kind),
            ((rows, width), (rows, width)),
            (),
            (*table, w, gains, *near),
            2 * group_products,
        )
        parts = []
        if step > 0:
            head = kernel_call(
                head_kernel,
                ((count, width),) * 3,
                (),
                (*table, w, gains, *state[:3]),
            )
            first, *queries, keys, values = kernel_call(
                own_kernel,
                ((count, width), (rows - count, width), (rows, width), (rows, width)),
                (window_start,),
                (*table, w, gains, near_keys, near_values, *head, *state),
                3 * group_products + attention_products,
                attention_products // HD,
            )
            parts = [first]
        for query in queries:
            rest = kernel_call(
                rest_kernel,
                (count, width),
                (window_start,),
                (after(query, *parts), keys, values, near_keys, near_values),
                attention_products,
                attention_products // HD,
            )
            parts.append(rest)
        received = [swap(part) for part in parts]
        waits = []
        if step < STEPS - 1:
            fresh_other = routed(
                after(fresh[step], near_keys if step else received[0]), lambda q, h: (last, 1 - h) if q == last - 2 else None
            )
            waits = [fresh_other] if step else []
        if step < STEPS - 1:
            bases = kernel_call(
                functools.partial(mine_kernel, kind),
                ((count, 2 * width),) * CHUNKS,
                (level_index,),
                (*table, w_out, *state, *parts),
                2 * out_products,
                dtype=jnp.float32,
            )
        else:
            bases = kernel_call(
                last_mine_kernel,
                ((count, width),) * CHUNKS,
                (),
                (rows_mine, w_out, *parts),
                out_products,
                dtype=jnp.float32,
            )
        received[0] = after(received[0], *bases, *waits)
        if step == 0:
            w_other = other_projection(piece, parts[0], w_out.shape)
        if step < STEPS - 1:
            new = []
            for n in range(CHUNKS):
                block = kernel_call(
                    project_kernel,
                    (count, 2 * width),
                    (level_index,),
                    (*table, w_other, bases[n], after(received[n], *new)),
                    out_products,
                )
                new.append(block)
            state = (fresh[step], fresh_other, *[down(block) for block in new])
            near_kind, near = "chunks", [after(block, state[2]) for block in new]
            kind = "fresh"
        else:
            done = []
            for n in range(CHUNKS):
                pair = kernel_call(
                    functools.partial(final_kernel, kind, n * count),
                    ((count, width), (count, width)),
                    (level_index,),
                    (rows_mine, w_other, bases[n], after(received[n], *(p[0] for p in done)), *state),
                    out_products // 2,
                )
                done.append(pair)
            advanced = [down(block) for block, _ in done]
            first = kernel_call(enter_kernel, (count, width), (), (advanced[0], fresh[step]))
            final, velocity = kernel_call(
                finish_kernel,
                ((rows, width), (rows, width)),
                (),
                (first, after(advanced[1], first), fresh[step], done[0][1], done[1][1]),
            )
    return (final, velocity)


def solution(mesh):
    placed = (
        P("queue", "heads"),
        P(None, None, "heads"),
        P(),
        P(),
        P(None, "heads"),
        P(None, "heads"),
        P(None, "heads"),
        P(None, None, "heads"),
        P("heads"),
        P("heads"),
        P("heads", None),
    )
    return jax.shard_map(
        on_device,
        mesh=mesh,
        in_specs=placed,
        out_specs=(P("queue", "heads"), P("queue", "heads")),
        check_vma=False,
    )
```

```python
import functools

import jax
import jax.numpy as jnp
from jax import lax
from jax.experimental import pallas as pl
from jax.experimental.pallas import tpu as pltpu
from jax.sharding import PartitionSpec as P

HD = 128
STEPS = 3
LEVELS = 64
EPS = 1e-06
AXES = ("queue", "heads")
VMEM_LIMIT = 24 * 1024 * 1024
CHUNKS = 2
SHIFT, SCALE, GATE, NEAR_SHIFT, NEAR_SCALE = range(5)
TABLE_ROWS = 16


def routed(block, target):
    slots, halves = lax.axis_size("queue"), lax.axis_size("heads")
    pairs = []
    for q in range(slots):
        for h in range(halves):
            to = target(q, h)
            if to is not None and 0 <= to[0] < slots:
                pairs.append((q * halves + h, to[0] * halves + to[1]))
    return lax.ppermute(block, AXES, pairs)


def dot(a, b):
    return jnp.dot(a, b, preferred_element_type=jnp.float32)


def dot_t(a, b):
    return lax.dot_general(a, b, (((1,), (1,)), ((), ())), preferred_element_type=jnp.float32)


def modulated(low, high, shift, scale):
    low, high = low.astype(jnp.float32), high.astype(jnp.float32)
    total = jnp.sum(low * low, axis=-1, keepdims=True) + jnp.sum(high * high, axis=-1, keepdims=True)
    factor = lax.rsqrt(total / (2 * low.shape[-1]) + EPS)
    parts = [low, high]
    for n in range(2):
        parts[n] = (parts[n] * factor * (1.0 + scale[n]) + shift[n]).astype(jnp.bfloat16)
    return jnp.concatenate(parts, axis=-1)


def normed(block, gain):
    mean = jnp.mean(block * block, axis=-1, keepdims=True)
    return (block * lax.rsqrt(mean + EPS) * gain).astype(jnp.bfloat16)


def ordered(mine, other):
    first = lax.axis_index("heads") == 0
    return jnp.where(first, mine, other), jnp.where(first, other, mine)


def table_row(rows, n):
    mine, other = (r[...].astype(jnp.float32)[n : n + 1, :] for r in rows)
    return ordered(mine, other)


def halves_of(kind, refs, row, count):
    if kind == "pair":
        return ordered(refs[0][row : row + count, :], refs[1][row : row + count, :])
    chunks = refs if kind == "chunks" else refs[2:]
    size = chunks[0].shape[0]
    wide = [c[...] for c in chunks[row // size : (row + count) // size]]
    wide = wide[0] if len(wide) == 1 else jnp.concatenate(wide, axis=0)
    width = wide.shape[1] // 2
    low, high = wide[:, :width], wide[:, width:]
    if kind == "chunks":
        return low, high
    passed = ordered(*(group[row : row + count, :] for group in refs[:2]))
    last = lax.axis_index("queue") == lax.axis_size("queue") - 1
    return jnp.where(last, passed[0], low), jnp.where(last, passed[1], high)


def rows_kernel(levels_hbm, shift_hbm, scale_hbm, gate_hbm, rows, levels, shift, scale, gate, arrived):
    tables = ((levels_hbm, levels), (shift_hbm, shift), (scale_hbm, scale), (gate_hbm, gate))
    copies = [pltpu.make_async_copy(a, b, arrived.at[n]) for n, (a, b) in enumerate(tables)]
    for copy in copies:
        copy.start()
    for copy in copies:
        copy.wait()
    position = lax.axis_index("queue")
    level = levels[position]
    below = levels[jnp.maximum(position - 1, 0)]
    shape = (TABLE_ROWS, shift.shape[0])
    row = lax.broadcasted_iota(jnp.int32, shape, 0)
    column = lax.broadcasted_iota(jnp.int32, shape, 1)

    def picked(table, own, near):
        chosen = jnp.logical_and(row == own, column == level)
        if near is not None:
            chosen = jnp.logical_or(chosen, jnp.logical_and(row == near, column == below))
        return dot(jnp.where(chosen, 1.0, 0.0).astype(jnp.bfloat16), table[...])

    out = picked(shift, SHIFT, NEAR_SHIFT) + picked(scale, SCALE, NEAR_SCALE)
    rows[...] = (out + picked(gate, GATE, None)).astype(jnp.bfloat16)


def rows_call(levels, tables):
    held = [pltpu.VMEM(table.shape, table.dtype) for table in tables]
    return pl.pallas_call(
        rows_kernel,
        out_shape=jax.ShapeDtypeStruct((TABLE_ROWS, tables[0].shape[1]), jnp.bfloat16),
        in_specs=[pl.BlockSpec(memory_space=pl.ANY)] * (1 + len(tables)),
        out_specs=pl.BlockSpec(memory_space=pltpu.VMEM),
        scratch_shapes=[pltpu.SMEM(levels.shape, levels.dtype)] + held + [pltpu.SemaphoreType.DMA((1 + len(tables),))],
        compiler_params=pltpu.CompilerParams(vmem_limit_bytes=VMEM_LIMIT),
    )(*(pltpu.with_memory_space_constraint(a, pltpu.HBM) for a in (levels, *tables)))


def stage_kernel(w_hbm, q_hbm, k_hbm, fresh_hbm, w_out_hbm, w, gains, *refs):
    *fresh, w_out, q_gain, k_gain, arrived = refs
    moves = [(w_hbm, w), (q_hbm, q_gain), (k_hbm, k_gain), (w_out_hbm, w_out)]
    moves += [(fresh_hbm.at[n], group) for n, group in enumerate(fresh)]
    copies = [pltpu.make_async_copy(a, b, arrived.at[n]) for n, (a, b) in enumerate(moves)]
    for copy in copies:
        copy.start()
    for copy in copies:
        copy.wait()
    gains[0:1, :] = q_gain[...].reshape(1, -1)
    gains[1:2, :] = k_gain[...].reshape(1, -1)


def stage_call(w, q_gain, k_gain, fresh, w_out):
    vmem = pl.BlockSpec(memory_space=pltpu.VMEM)
    held = [pltpu.with_memory_space_constraint(a, pltpu.HBM) for a in (w, q_gain, k_gain, fresh, w_out)]
    groups = [pltpu.VMEM(fresh.shape[1:], fresh.dtype)] * STEPS
    return pl.pallas_call(
        stage_kernel,
        out_shape=(
            pltpu.VMEM(w.shape, w.dtype),
            pltpu.VMEM((2, q_gain.shape[0]), q_gain.dtype),
            *groups,
            pltpu.VMEM(w_out.shape, w_out.dtype),
        ),
        in_specs=[pl.BlockSpec(memory_space=pl.ANY)] * 5,
        out_specs=(vmem,) * (3 + len(groups)),
        scratch_shapes=[
            pltpu.VMEM(q_gain.shape, q_gain.dtype),
            pltpu.VMEM(k_gain.shape, k_gain.dtype),
            pltpu.SemaphoreType.DMA((4 + len(groups),)),
        ],
        compiler_params=pltpu.CompilerParams(vmem_limit_bytes=VMEM_LIMIT),
    )(*held)


def near_kernel(kind, rows_mine, rows_other, w, gains, *refs):
    x, (keys, values) = refs[:-2], refs[-2:]
    width = w.shape[2]
    table = (rows_mine, rows_other)
    low, high = halves_of(kind, x, 0, keys.shape[0])
    moved = modulated(low, high, table_row(table, NEAR_SHIFT), table_row(table, NEAR_SCALE))
    raw = dot(moved, w[1])
    gain = gains[1:2, :]
    for a in range(0, width, HD):
        keys[:, a : a + HD] = normed(raw[:, a : a + HD], gain[:, a : a + HD])
    values[...] = dot(moved, w[2]).astype(jnp.bfloat16)


def attend(starts, attended, queries, keys, values, near_keys, near_values):
    position = lax.axis_index("queue")
    rows = values.shape[0]
    start = jnp.where(position > 0, starts[position], rows)
    visible = lax.broadcasted_iota(jnp.int32, (1, rows), 1) >= start
    factor = 1.4426950408889634 / (HD**0.5)
    parts = [slice(a, a + HD) for a in range(0, values.shape[1], HD)]
    scores = []
    for n, part in enumerate(parts):
        near = jnp.where(visible, dot_t(queries[n], near_keys[:, part]), jnp.float32(-1e30))
        scores.append((dot_t(queries[n], keys[n]), near))
    tops = [jnp.max(jnp.maximum(own, near), axis=-1, keepdims=True) for own, near in scores]
    weights = [
        (jnp.exp2((own - top) * factor), jnp.exp2((near - top) * factor))
        for (own, near), top in zip(scores, tops)
    ]
    totals = [jnp.sum(own + near, axis=-1, keepdims=True) for own, near in weights]
    for part, (own, near), total in zip(parts, weights, totals):
        out = dot(own.astype(jnp.bfloat16), values[:, part])
        out = out + dot(near.astype(jnp.bfloat16), near_values[:, part])
        attended[:, part] = (out / total).astype(jnp.bfloat16)


def projected(low, high, table, w, gains):
    width = w.shape[2]
    moved = modulated(low, high, table_row(table, SHIFT), table_row(table, SCALE))
    query_raw = dot(moved, w[0])
    key_raw = dot(moved, w[1])
    values = dot(moved, w[2]).astype(jnp.bfloat16)
    parts = [slice(a, a + HD) for a in range(0, width, HD)]
    queries = [normed(query_raw[:, part], gains[0:1, part]) for part in parts]
    keys = [normed(key_raw[:, part], gains[1:2, part]) for part in parts]
    return queries, keys, values


def head_kernel(rows_mine, rows_other, w, gains, fresh, fresh_other, chunk, queries, keys, values):
    low, high = halves_of("fresh", (fresh, fresh_other, chunk), 0, chunk.shape[0])
    heads, key_heads, value = projected(low, high, (rows_mine, rows_other), w, gains)
    values[...] = value
    for n in range(len(heads)):
        queries[:, n * HD : (n + 1) * HD] = heads[n]
        keys[:, n * HD : (n + 1) * HD] = key_heads[n]


def own_kernel(
    starts, rows_mine, rows_other, w, gains, near_keys, near_values, first_queries, first_keys, first_values,
    fresh, fresh_other, first, rest, attended, queries, keys, values,
):
    count = rest.shape[0]
    low, high = halves_of("fresh", (fresh, fresh_other, first, rest), count, count)
    heads, key_heads, value = projected(low, high, (rows_mine, rows_other), w, gains)
    values[:count, :] = first_values[...]
    values[count:, :] = value
    keys[:count, :] = first_keys[...]
    first_heads, all_keys = [], []
    for n in range(len(heads)):
        part = slice(n * HD, (n + 1) * HD)
        queries[:, part] = heads[n]
        keys[count:, part] = key_heads[n]
        first_heads.append(first_queries[:, part])
        all_keys.append(keys[:, part])
    attend(starts, attended, first_heads, all_keys, values, near_keys, near_values)


def qkv_kernel(rows_mine, rows_other, w, gains, mine, other, *refs):
    *queries, keys, values = refs
    low, high = halves_of("pair", (mine, other), 0, keys.shape[0])
    heads, key_heads, value = projected(low, high, (rows_mine, rows_other), w, gains)
    values[...] = value
    for n in range(len(heads)):
        part = slice(n * HD, (n + 1) * HD)
        keys[:, part] = key_heads[n]
        for c, chunk in enumerate(queries):
            chunk[:, part] = heads[n][c * chunk.shape[0] : (c + 1) * chunk.shape[0]]


def rest_kernel(starts, queries, keys, values, near_keys, near_values, attended):
    parts = [slice(a, a + HD) for a in range(0, attended.shape[1], HD)]
    query_heads = [queries[:, part] for part in parts]
    key_heads = [keys[:, part] for part in parts]
    attend(starts, attended, query_heads, key_heads, values, near_keys, near_values)


def step_size_of(levels):
    position = lax.axis_index("queue")
    level = levels[position]
    below = levels[jnp.maximum(position - 1, 0)]
    t_cur = (level.astype(jnp.float32) + 1.0) / LEVELS
    t_next = jnp.where(position > 0, (below.astype(jnp.float32) + 1.0) / LEVELS, jnp.float32(0.0))
    return t_next - t_cur


def mine_kernel(kind, levels, rows_mine, rows_other, w_mine, *refs):
    x, chunks, bases = refs[: -2 * CHUNKS], refs[-2 * CHUNKS : -CHUNKS], refs[-CHUNKS:]
    gate = table_row((rows_mine, rows_other), GATE)
    size = step_size_of(levels)
    for c, (chunk, base) in enumerate(zip(chunks, bases)):
        count, width = chunk.shape[0], base.shape[1] // 2
        halves = halves_of(kind, x, c * count, count)
        product = dot(chunk[...], w_mine[...])
        for n in range(2):
            part = slice(n * width, (n + 1) * width)
            base[:, part] = halves[n].astype(jnp.float32) + size * gate[n] * product[:, part]


def project_kernel(levels, rows_mine, rows_other, w_other, base, a_other, new):
    width = new.shape[1] // 2
    gate = table_row((rows_mine, rows_other), GATE)
    size = step_size_of(levels)
    product = dot(a_other[...], w_other[...])
    for n in range(2):
        part = slice(n * width, (n + 1) * width)
        new[:, part] = (base[:, part] + size * gate[n] * product[:, part]).astype(jnp.bfloat16)


def own_features(width):
    return pl.ds(pl.multiple_of(lax.axis_index("heads") * width, HD), width)


def last_mine_kernel(rows_mine, w_mine, *refs):
    gate = rows_mine[...].astype(jnp.float32)[GATE : GATE + 1, :]
    for chunk, base in zip(refs[:CHUNKS], refs[CHUNKS:]):
        base[...] = gate * dot(chunk[...], w_mine[:, own_features(base.shape[1])])


def final_kernel(kind, row, levels, rows_mine, w_other, base, a_other, *refs):
    x, (new, velocity_out) = refs[:-2], refs[-2:]
    count, width = new.shape
    low, high = halves_of(kind, x, row, count)
    held = jnp.where(lax.axis_index("heads") == 0, low, high).astype(jnp.float32)
    gate = rows_mine[...].astype(jnp.float32)[GATE : GATE + 1, :]
    velocity = base[...] + gate * dot(a_other[...], w_other[:, own_features(width)])
    velocity_out[...] = velocity.astype(jnp.bfloat16)
    new[...] = (held + step_size_of(levels) * velocity).astype(jnp.bfloat16)


def entering(advanced, fresh):
    last = lax.axis_index("queue") == lax.axis_size("queue") - 1
    return jnp.where(last, fresh, advanced)


def enter_kernel(advanced, fresh, out):
    out[...] = entering(advanced[...], fresh[: out.shape[0], :])


def finish_kernel(first, advanced, fresh, velocity_first, velocity_rest, final, velocity):
    count = first.shape[0]
    final[:count, :] = first[...]
    final[count:, :] = entering(advanced[...], fresh[count:, :])
    velocity[:count, :] = velocity_first[...]
    velocity[count:, :] = velocity_rest[...]


def piece_of(position):
    core = position % 2
    z = (position // 4) % 8
    y = position // 32
    return (y + 2 * z) % 4, core


def gather_kernel(own, back, ahead, across, others, w_other):
    group, core = piece_of(lax.axis_index("queue"))
    size = own.shape[0]
    for n, (block, turn) in enumerate(((own, 0), (back, 3), (ahead, 1), (across, 2))):
        place = (group + turn) % 4 * 2
        w_other[pl.ds(pl.multiple_of((place + core) * size, 16), size), :] = block[...]
        w_other[pl.ds(pl.multiple_of((place + 1 - core) * size, 16), size), :] = others[n]


def kernel_call(kernel, out, scalars, arrays, products=0, exponentials=0, dtype=jnp.bfloat16):
    many = isinstance(out[0], tuple)
    outs = out if many else (out,)
    shapes = tuple(jax.ShapeDtypeStruct(s, dtype) for s in outs)
    size = sum(a.size * a.dtype.itemsize for a in arrays)
    result = pl.pallas_call(
        kernel,
        cost_estimate=pl.CostEstimate(
            flops=2 * products, bytes_accessed=size, transcendentals=exponentials
        ),
        out_shape=shapes,
        in_specs=[pl.BlockSpec(memory_space=pltpu.SMEM)] * len(scalars)
        + [pl.BlockSpec(memory_space=pltpu.VMEM)] * len(arrays),
        out_specs=tuple([pl.BlockSpec(memory_space=pltpu.VMEM)] * len(outs)),
        compiler_params=pltpu.CompilerParams(vmem_limit_bytes=VMEM_LIMIT),
    )(*scalars, *arrays)
    return result if many else result[0]


def after(block, *others):
    return lax.optimization_barrier((block, *others))[0]


def fetched_piece(w_out):
    size = w_out.shape[0] // 8
    group, core = piece_of(lax.axis_index("queue"))
    return lax.dynamic_slice_in_dim(w_out, (group * 2 + core) * size, size, 0)


def other_projection(own, ready, shape):
    def turned(y, z):
        return lambda q, h: ((q // 32 + y) % 4 * 32 + (q // 4 + z) % 8 * 4 + q % 4, h)

    back = routed(own, turned(1, 0))
    ahead = routed(own, turned(-1, 0))
    across = routed(own, turned(0, -1))
    own, back, ahead, across, _ = lax.optimization_barrier((own, back, ahead, across, ready))
    others = routed(jnp.stack([own, back, ahead, across]), lambda q, h: (q ^ 1, h))
    return kernel_call(gather_kernel, shape, (), (own, back, ahead, across, others))


def on_device(
    frames,
    fresh_groups,
    level_index,
    window_start,
    mod_shift,
    mod_scale,
    mod_gate,
    w_qkv,
    q_gain,
    k_gain,
    w_out,
):
    last = lax.axis_size("queue") - 1
    rows, width = frames.shape
    count = rows // CHUNKS
    w = jnp.transpose(w_qkv, (1, 0, 2))
    group_products = rows * w.shape[1] * width
    attention_products = 4 * count * rows * width
    out_products = 2 * count * width * width

    def swap(block):
        return routed(block, lambda q, h: (q, 1 - h))

    def up(block):
        return routed(block, lambda q, h: (q + 1, h))

    def down(block):
        return routed(block, lambda q, h: (q - 1, h))

    other = swap(frames)
    rows_mine = rows_call(level_index, (mod_shift, mod_scale, mod_gate))
    rows_other = swap(rows_mine)
    w_out_hbm = w_out
    w, gains, *fresh, w_out = stage_call(w, q_gain, k_gain, fresh_groups, w_out)
    near_mine = up(after(frames, other))
    near_other = up(after(other, rows_other, gains))
    piece = routed(after(fetched_piece(w_out_hbm), rows_mine), lambda q, h: (q ^ 2, 1 - h))
    table = (rows_mine, rows_other)
    kind, state = "pair", (frames, other)
    near_kind, near = "pair", (near_mine, near_other)
    *queries, keys, values = kernel_call(
        qkv_kernel,
        ((count, width),) * CHUNKS + ((rows, width),) * 2,
        (),
        (*table, w, gains, *state),
        3 * group_products,
    )
    near = (near_mine, after(near_other, keys))
    for step in range(STEPS):
        near_keys, near_values = kernel_call(
            functools.partial(near_kernel, near_kind),
            ((rows, width), (rows, width)),
            (),
            (*table, w, gains, *near),
            2 * group_products,
        )
        parts = []
        if step > 0:
            head = kernel_call(
                head_kernel,
                ((count, width),) * 3,
                (),
                (*table, w, gains, *state[:3]),
            )
            first, *queries, keys, values = kernel_call(
                own_kernel,
                ((count, width), (rows - count, width), (rows, width), (rows, width)),
                (window_start,),
                (*table, w, gains, near_keys, near_values, *head, *state),
                3 * group_products + attention_products,
                attention_products // HD,
            )
            parts = [first]
        for query in queries:
            rest = kernel_call(
                rest_kernel,
                (count, width),
                (window_start,),
                (after(query, *parts), keys, values, near_keys, near_values),
                attention_products,
                attention_products // HD,
            )
            parts.append(rest)
        received = [swap(part) for part in parts]
        waits = []
        if step < STEPS - 1:
            fresh_other = routed(
                after(fresh[step], near_keys if step else received[0]), lambda q, h: (last, 1 - h) if q == last - 2 else None
            )
            waits = [fresh_other] if step else []
        if step < STEPS - 1:
            bases = kernel_call(
                functools.partial(mine_kernel, kind),
                ((count, 2 * width),) * CHUNKS,
                (level_index,),
                (*table, w_out, *state, *parts),
                2 * out_products,
                dtype=jnp.float32,
            )
        else:
            bases = kernel_call(
                last_mine_kernel,
                ((count, width),) * CHUNKS,
                (),
                (rows_mine, w_out, *parts),
                out_products,
                dtype=jnp.float32,
            )
        received[0] = after(received[0], *bases, *waits)
        if step == 0:
            w_other = other_projection(piece, parts[1], w_out.shape)
        if step < STEPS - 1:
            new = []
            for n in range(CHUNKS):
                block = kernel_call(
                    project_kernel,
                    (count, 2 * width),
                    (level_index,),
                    (*table, w_other, bases[n], after(received[n], *new)),
                    out_products,
                )
                new.append(block)
            state = (fresh[step], fresh_other, *[down(block) for block in new])
            near_kind, near = "chunks", [after(block, state[2]) for block in new]
            kind = "fresh"
        else:
            done = []
            for n in range(CHUNKS):
                pair = kernel_call(
                    functools.partial(final_kernel, kind, n * count),
                    ((count, width), (count, width)),
                    (level_index,),
                    (rows_mine, w_other, bases[n], after(received[n], *(p[0] for p in done)), *state),
                    out_products // 2,
                )
                done.append(pair)
            advanced = [down(block) for block, _ in done]
            first = kernel_call(enter_kernel, (count, width), (), (advanced[0], fresh[step]))
            final, velocity = kernel_call(
                finish_kernel,
                ((rows, width), (rows, width)),
                (),
                (first, after(advanced[1], first), fresh[step], done[0][1], done[1][1]),
            )
    return (final, velocity)


def solution(mesh):
    placed = (
        P("queue", "heads"),
        P(None, None, "heads"),
        P(),
        P(),
        P(None, "heads"),
        P(None, "heads"),
        P(None, "heads"),
        P(None, None, "heads"),
        P("heads"),
        P("heads"),
        P("heads", None),
    )
    return jax.shard_map(
        on_device,
        mesh=mesh,
        in_specs=placed,
        out_specs=(P("queue", "heads"), P("queue", "heads")),
        check_vma=False,
    )
```

```python
import functools

import jax
import jax.numpy as jnp
from jax import lax
from jax.experimental import pallas as pl
from jax.experimental.pallas import tpu as pltpu
from jax.sharding import PartitionSpec as P

HD = 128
STEPS = 3
LEVELS = 64
EPS = 1e-06
AXES = ("queue", "heads")
VMEM_LIMIT = 24 * 1024 * 1024
CHUNKS = 2
SHIFT, SCALE, GATE, NEAR_SHIFT, NEAR_SCALE = range(5)
TABLE_ROWS = 16


def routed(block, target):
    slots, halves = lax.axis_size("queue"), lax.axis_size("heads")
    pairs = []
    for q in range(slots):
        for h in range(halves):
            to = target(q, h)
            if to is not None and 0 <= to[0] < slots:
                pairs.append((q * halves + h, to[0] * halves + to[1]))
    return lax.ppermute(block, AXES, pairs)


def dot(a, b):
    return jnp.dot(a, b, preferred_element_type=jnp.float32)


def dot_t(a, b):
    return lax.dot_general(a, b, (((1,), (1,)), ((), ())), preferred_element_type=jnp.float32)


def modulated(low, high, shift, scale):
    low, high = low.astype(jnp.float32), high.astype(jnp.float32)
    total = jnp.sum(low * low, axis=-1, keepdims=True) + jnp.sum(high * high, axis=-1, keepdims=True)
    factor = lax.rsqrt(total / (2 * low.shape[-1]) + EPS)
    parts = [low, high]
    for n in range(2):
        parts[n] = (parts[n] * factor * (1.0 + scale[n]) + shift[n]).astype(jnp.bfloat16)
    return jnp.concatenate(parts, axis=-1)


def normed(block, gain):
    mean = jnp.mean(block * block, axis=-1, keepdims=True)
    return (block * lax.rsqrt(mean + EPS) * gain).astype(jnp.bfloat16)


def ordered(mine, other):
    first = lax.axis_index("heads") == 0
    return jnp.where(first, mine, other), jnp.where(first, other, mine)


def table_row(rows, n):
    mine, other = (r[...].astype(jnp.float32)[n : n + 1, :] for r in rows)
    return ordered(mine, other)


def halves_of(kind, refs, row, count):
    if kind == "pair":
        return ordered(refs[0][row : row + count, :], refs[1][row : row + count, :])
    chunks = refs if kind == "chunks" else refs[2:]
    size = chunks[0].shape[0]
    wide = [c[...] for c in chunks[row // size : (row + count) // size]]
    wide = wide[0] if len(wide) == 1 else jnp.concatenate(wide, axis=0)
    width = wide.shape[1] // 2
    low, high = wide[:, :width], wide[:, width:]
    if kind == "chunks":
        return low, high
    passed = ordered(*(group[row : row + count, :] for group in refs[:2]))
    last = lax.axis_index("queue") == lax.axis_size("queue") - 1
    return jnp.where(last, passed[0], low), jnp.where(last, passed[1], high)


def rows_kernel(levels_hbm, shift_hbm, scale_hbm, gate_hbm, rows, levels, shift, scale, gate, arrived):
    tables = ((levels_hbm, levels), (shift_hbm, shift), (scale_hbm, scale), (gate_hbm, gate))
    copies = [pltpu.make_async_copy(a, b, arrived.at[n]) for n, (a, b) in enumerate(tables)]
    for copy in copies:
        copy.start()
    for copy in copies:
        copy.wait()
    position = lax.axis_index("queue")
    level = levels[position]
    below = levels[jnp.maximum(position - 1, 0)]
    shape = (TABLE_ROWS, shift.shape[0])
    row = lax.broadcasted_iota(jnp.int32, shape, 0)
    column = lax.broadcasted_iota(jnp.int32, shape, 1)

    def picked(table, own, near):
        chosen = jnp.logical_and(row == own, column == level)
        if near is not None:
            chosen = jnp.logical_or(chosen, jnp.logical_and(row == near, column == below))
        return dot(jnp.where(chosen, 1.0, 0.0).astype(jnp.bfloat16), table[...])

    out = picked(shift, SHIFT, NEAR_SHIFT) + picked(scale, SCALE, NEAR_SCALE)
    rows[...] = (out + picked(gate, GATE, None)).astype(jnp.bfloat16)


def rows_call(levels, tables):
    held = [pltpu.VMEM(table.shape, table.dtype) for table in tables]
    return pl.pallas_call(
        rows_kernel,
        out_shape=jax.ShapeDtypeStruct((TABLE_ROWS, tables[0].shape[1]), jnp.bfloat16),
        in_specs=[pl.BlockSpec(memory_space=pl.ANY)] * (1 + len(tables)),
        out_specs=pl.BlockSpec(memory_space=pltpu.VMEM),
        scratch_shapes=[pltpu.SMEM(levels.shape, levels.dtype)] + held + [pltpu.SemaphoreType.DMA((1 + len(tables),))],
        compiler_params=pltpu.CompilerParams(vmem_limit_bytes=VMEM_LIMIT),
    )(*(pltpu.with_memory_space_constraint(a, pltpu.HBM) for a in (levels, *tables)))


def stage_kernel(w_hbm, q_hbm, k_hbm, fresh_hbm, w_out_hbm, w, gains, *refs):
    *fresh, w_out, q_gain, k_gain, arrived = refs
    moves = [(w_hbm, w), (q_hbm, q_gain), (k_hbm, k_gain), (w_out_hbm, w_out)]
    moves += [(fresh_hbm.at[n], group) for n, group in enumerate(fresh)]
    copies = [pltpu.make_async_copy(a, b, arrived.at[n]) for n, (a, b) in enumerate(moves)]
    for copy in copies:
        copy.start()
    for copy in copies:
        copy.wait()
    gains[0:1, :] = q_gain[...].reshape(1, -1)
    gains[1:2, :] = k_gain[...].reshape(1, -1)


def stage_call(w, q_gain, k_gain, fresh, w_out):
    vmem = pl.BlockSpec(memory_space=pltpu.VMEM)
    held = [pltpu.with_memory_space_constraint(a, pltpu.HBM) for a in (w, q_gain, k_gain, fresh, w_out)]
    groups = [pltpu.VMEM(fresh.shape[1:], fresh.dtype)] * STEPS
    return pl.pallas_call(
        stage_kernel,
        out_shape=(
            pltpu.VMEM(w.shape, w.dtype),
            pltpu.VMEM((2, q_gain.shape[0]), q_gain.dtype),
            *groups,
            pltpu.VMEM(w_out.shape, w_out.dtype),
        ),
        in_specs=[pl.BlockSpec(memory_space=pl.ANY)] * 5,
        out_specs=(vmem,) * (3 + len(groups)),
        scratch_shapes=[
            pltpu.VMEM(q_gain.shape, q_gain.dtype),
            pltpu.VMEM(k_gain.shape, k_gain.dtype),
            pltpu.SemaphoreType.DMA((4 + len(groups),)),
        ],
        compiler_params=pltpu.CompilerParams(vmem_limit_bytes=VMEM_LIMIT),
    )(*held)


def near_kernel(kind, rows_mine, rows_other, w, gains, *refs):
    x, (keys, values) = refs[:-2], refs[-2:]
    width = w.shape[2]
    table = (rows_mine, rows_other)
    low, high = halves_of(kind, x, 0, keys.shape[0])
    moved = modulated(low, high, table_row(table, NEAR_SHIFT), table_row(table, NEAR_SCALE))
    raw = dot(moved, w[1])
    gain = gains[1:2, :]
    for a in range(0, width, HD):
        keys[:, a : a + HD] = normed(raw[:, a : a + HD], gain[:, a : a + HD])
    values[...] = dot(moved, w[2]).astype(jnp.bfloat16)


def attend(starts, attended, queries, keys, values, near_keys, near_values):
    position = lax.axis_index("queue")
    rows = values.shape[0]
    start = jnp.where(position > 0, starts[position], rows)
    visible = lax.broadcasted_iota(jnp.int32, (1, rows), 1) >= start
    factor = 1.4426950408889634 / (HD**0.5)
    parts = [slice(a, a + HD) for a in range(0, values.shape[1], HD)]
    scores = []
    for n, part in enumerate(parts):
        near = jnp.where(visible, dot_t(queries[n], near_keys[:, part]), jnp.float32(-1e30))
        scores.append((dot_t(queries[n], keys[n]), near))
    tops = [jnp.max(jnp.maximum(own, near), axis=-1, keepdims=True) for own, near in scores]
    weights = [
        (jnp.exp2((own - top) * factor), jnp.exp2((near - top) * factor))
        for (own, near), top in zip(scores, tops)
    ]
    totals = [jnp.sum(own + near, axis=-1, keepdims=True) for own, near in weights]
    for part, (own, near), total in zip(parts, weights, totals):
        out = dot(own.astype(jnp.bfloat16), values[:, part])
        out = out + dot(near.astype(jnp.bfloat16), near_values[:, part])
        attended[:, part] = (out / total).astype(jnp.bfloat16)


def projected(low, high, table, w, gains):
    width = w.shape[2]
    moved = modulated(low, high, table_row(table, SHIFT), table_row(table, SCALE))
    query_raw = dot(moved, w[0])
    key_raw = dot(moved, w[1])
    values = dot(moved, w[2]).astype(jnp.bfloat16)
    parts = [slice(a, a + HD) for a in range(0, width, HD)]
    queries = [normed(query_raw[:, part], gains[0:1, part]) for part in parts]
    keys = [normed(key_raw[:, part], gains[1:2, part]) for part in parts]
    return queries, keys, values


def head_kernel(rows_mine, rows_other, w, gains, fresh, fresh_other, chunk, queries, keys, values):
    low, high = halves_of("fresh", (fresh, fresh_other, chunk), 0, chunk.shape[0])
    heads, key_heads, value = projected(low, high, (rows_mine, rows_other), w, gains)
    values[...] = value
    for n in range(len(heads)):
        queries[:, n * HD : (n + 1) * HD] = heads[n]
        keys[:, n * HD : (n + 1) * HD] = key_heads[n]


def own_kernel(
    starts, rows_mine, rows_other, w, gains, near_keys, near_values, first_queries, first_keys, first_values,
    fresh, fresh_other, first, rest, attended, queries, keys, values,
):
    count = rest.shape[0]
    low, high = halves_of("fresh", (fresh, fresh_other, first, rest), count, count)
    heads, key_heads, value = projected(low, high, (rows_mine, rows_other), w, gains)
    values[:count, :] = first_values[...]
    values[count:, :] = value
    keys[:count, :] = first_keys[...]
    first_heads, all_keys = [], []
    for n in range(len(heads)):
        part = slice(n * HD, (n + 1) * HD)
        queries[:, part] = heads[n]
        keys[count:, part] = key_heads[n]
        first_heads.append(first_queries[:, part])
        all_keys.append(keys[:, part])
    attend(starts, attended, first_heads, all_keys, values, near_keys, near_values)


def qkv_kernel(rows_mine, rows_other, w, gains, mine, other, *refs):
    *queries, keys, values = refs
    low, high = halves_of("pair", (mine, other), 0, keys.shape[0])
    heads, key_heads, value = projected(low, high, (rows_mine, rows_other), w, gains)
    values[...] = value
    for n in range(len(heads)):
        part = slice(n * HD, (n + 1) * HD)
        keys[:, part] = key_heads[n]
        for c, chunk in enumerate(queries):
            chunk[:, part] = heads[n][c * chunk.shape[0] : (c + 1) * chunk.shape[0]]


def rest_kernel(starts, queries, keys, values, near_keys, near_values, attended):
    parts = [slice(a, a + HD) for a in range(0, attended.shape[1], HD)]
    query_heads = [queries[:, part] for part in parts]
    key_heads = [keys[:, part] for part in parts]
    attend(starts, attended, query_heads, key_heads, values, near_keys, near_values)


def step_size_of(levels):
    position = lax.axis_index("queue")
    level = levels[position]
    below = levels[jnp.maximum(position - 1, 0)]
    t_cur = (level.astype(jnp.float32) + 1.0) / LEVELS
    t_next = jnp.where(position > 0, (below.astype(jnp.float32) + 1.0) / LEVELS, jnp.float32(0.0))
    return t_next - t_cur


def mine_kernel(kind, levels, rows_mine, rows_other, w_mine, *refs):
    x, chunks, bases = refs[: -2 * CHUNKS], refs[-2 * CHUNKS : -CHUNKS], refs[-CHUNKS:]
    gate = table_row((rows_mine, rows_other), GATE)
    size = step_size_of(levels)
    for c, (chunk, base) in enumerate(zip(chunks, bases)):
        count, width = chunk.shape[0], base.shape[1] // 2
        halves = halves_of(kind, x, c * count, count)
        product = dot(chunk[...], w_mine[...])
        for n in range(2):
            part = slice(n * width, (n + 1) * width)
            base[:, part] = halves[n].astype(jnp.float32) + size * gate[n] * product[:, part]


def project_kernel(levels, rows_mine, rows_other, w_other, base, a_other, new):
    width = new.shape[1] // 2
    gate = table_row((rows_mine, rows_other), GATE)
    size = step_size_of(levels)
    product = dot(a_other[...], w_other[...])
    for n in range(2):
        part = slice(n * width, (n + 1) * width)
        new[:, part] = (base[:, part] + size * gate[n] * product[:, part]).astype(jnp.bfloat16)


def own_features(width):
    return pl.ds(pl.multiple_of(lax.axis_index("heads") * width, HD), width)


def last_mine_kernel(rows_mine, w_mine, *refs):
    gate = rows_mine[...].astype(jnp.float32)[GATE : GATE + 1, :]
    for chunk, base in zip(refs[:CHUNKS], refs[CHUNKS:]):
        base[...] = gate * dot(chunk[...], w_mine[:, own_features(base.shape[1])])


def final_kernel(kind, row, levels, rows_mine, w_other, base, a_other, *refs):
    x, (new, velocity_out) = refs[:-2], refs[-2:]
    count, width = new.shape
    low, high = halves_of(kind, x, row, count)
    held = jnp.where(lax.axis_index("heads") == 0, low, high).astype(jnp.float32)
    gate = rows_mine[...].astype(jnp.float32)[GATE : GATE + 1, :]
    velocity = base[...] + gate * dot(a_other[...], w_other[:, own_features(width)])
    velocity_out[...] = velocity.astype(jnp.bfloat16)
    new[...] = (held + step_size_of(levels) * velocity).astype(jnp.bfloat16)


def entering(advanced, fresh):
    last = lax.axis_index("queue") == lax.axis_size("queue") - 1
    return jnp.where(last, fresh, advanced)


def enter_kernel(advanced, fresh, out):
    out[...] = entering(advanced[...], fresh[: out.shape[0], :])


def finish_kernel(first, advanced, fresh, velocity_first, velocity_rest, final, velocity):
    count = first.shape[0]
    final[:count, :] = first[...]
    final[count:, :] = entering(advanced[...], fresh[count:, :])
    velocity[:count, :] = velocity_first[...]
    velocity[count:, :] = velocity_rest[...]


def piece_of(position):
    core = position % 2
    z = (position // 4) % 8
    y = position // 32
    return (y + 2 * z) % 4, core


def gather_kernel(own, back, ahead, across, others, w_other):
    group, core = piece_of(lax.axis_index("queue"))
    size = own.shape[0]
    for n, (block, turn) in enumerate(((own, 0), (back, 3), (ahead, 1), (across, 2))):
        place = (group + turn) % 4 * 2
        w_other[pl.ds(pl.multiple_of((place + core) * size, 16), size), :] = block[...]
        w_other[pl.ds(pl.multiple_of((place + 1 - core) * size, 16), size), :] = others[n]


def kernel_call(kernel, out, scalars, arrays, products=0, exponentials=0, dtype=jnp.bfloat16):
    many = isinstance(out[0], tuple)
    outs = out if many else (out,)
    shapes = tuple(jax.ShapeDtypeStruct(s, dtype) for s in outs)
    size = sum(a.size * a.dtype.itemsize for a in arrays)
    result = pl.pallas_call(
        kernel,
        cost_estimate=pl.CostEstimate(
            flops=2 * products, bytes_accessed=size, transcendentals=exponentials
        ),
        out_shape=shapes,
        in_specs=[pl.BlockSpec(memory_space=pltpu.SMEM)] * len(scalars)
        + [pl.BlockSpec(memory_space=pltpu.VMEM)] * len(arrays),
        out_specs=tuple([pl.BlockSpec(memory_space=pltpu.VMEM)] * len(outs)),
        compiler_params=pltpu.CompilerParams(vmem_limit_bytes=VMEM_LIMIT),
    )(*scalars, *arrays)
    return result if many else result[0]


def after(block, *others):
    return lax.optimization_barrier((block, *others))[0]


def fetched_piece(w_out):
    size = w_out.shape[0] // 8
    group, core = piece_of(lax.axis_index("queue"))
    return lax.dynamic_slice_in_dim(w_out, (group * 2 + core) * size, size, 0)


def other_projection(own, ready, shape):
    def turned(y, z):
        return lambda q, h: ((q // 32 + y) % 4 * 32 + (q // 4 + z) % 8 * 4 + q % 4, h)

    back = routed(own, turned(1, 0))
    ahead = routed(own, turned(-1, 0))
    across = routed(own, turned(0, -1))
    own, back, ahead, across, _ = lax.optimization_barrier((own, back, ahead, across, ready))
    others = routed(jnp.stack([own, back, ahead, across]), lambda q, h: (q ^ 1, h))
    return kernel_call(gather_kernel, shape, (), (own, back, ahead, across, others))


def on_device(
    frames,
    fresh_groups,
    level_index,
    window_start,
    mod_shift,
    mod_scale,
    mod_gate,
    w_qkv,
    q_gain,
    k_gain,
    w_out,
):
    last = lax.axis_size("queue") - 1
    rows, width = frames.shape
    count = rows // CHUNKS
    w = jnp.transpose(w_qkv, (1, 0, 2))
    group_products = rows * w.shape[1] * width
    attention_products = 4 * count * rows * width
    out_products = 2 * count * width * width

    def swap(block):
        return routed(block, lambda q, h: (q, 1 - h))

    def up(block):
        return routed(block, lambda q, h: (q + 1, h))

    def down(block):
        return routed(block, lambda q, h: (q - 1, h))

    other = swap(frames)
    rows_mine = rows_call(level_index, (mod_shift, mod_scale, mod_gate))
    rows_other = swap(rows_mine)
    w_out_hbm = w_out
    w, gains, *fresh, w_out = stage_call(w, q_gain, k_gain, fresh_groups, w_out)
    near_mine = up(after(frames, other))
    near_other = up(after(other, rows_other, gains))
    piece = routed(after(fetched_piece(w_out_hbm), rows_mine), lambda q, h: (q ^ 2, 1 - h))
    table = (rows_mine, rows_other)
    kind, state = "pair", (frames, other)
    near_kind, near = "pair", (near_mine, near_other)
    *queries, keys, values = kernel_call(
        qkv_kernel,
        ((count, width),) * CHUNKS + ((rows, width),) * 2,
        (),
        (*table, w, gains, *state),
        3 * group_products,
    )
    near = (near_mine, after(near_other, keys))
    for step in range(STEPS):
        near_keys, near_values = kernel_call(
            functools.partial(near_kernel, near_kind),
            ((rows, width), (rows, width)),
            (),
            (*table, w, gains, *near),
            2 * group_products,
        )
        parts = []
        if step > 0:
            head = kernel_call(
                head_kernel,
                ((count, width),) * 3,
                (),
                (*table, w, gains, *state[:3]),
            )
            first, *queries, keys, values = kernel_call(
                own_kernel,
                ((count, width), (rows - count, width), (rows, width), (rows, width)),
                (window_start,),
                (*table, w, gains, near_keys, near_values, *head, *state),
                3 * group_products + attention_products,
                attention_products // HD,
            )
            parts = [first]
        for query in queries:
            rest = kernel_call(
                rest_kernel,
                (count, width),
                (window_start,),
                (after(query, *parts), keys, values, near_keys, near_values),
                attention_products,
                attention_products // HD,
            )
            parts.append(rest)
        received = [swap(part) for part in parts]
        waits = []
        if step < STEPS - 1:
            fresh_other = routed(
                after(fresh[step], near_keys if step else received[0]), lambda q, h: (last, 1 - h) if q == last - 2 else None
            )
            waits = [fresh_other] if step else []
        if step < STEPS - 1:
            bases = kernel_call(
                functools.partial(mine_kernel, kind),
                ((count, 2 * width),) * CHUNKS,
                (level_index,),
                (*table, w_out, *state, *parts),
                2 * out_products,
                dtype=jnp.float32,
            )
        else:
            bases = kernel_call(
                last_mine_kernel,
                ((count, width),) * CHUNKS,
                (),
                (rows_mine, w_out, *parts),
                out_products,
                dtype=jnp.float32,
            )
            received[1] = swap(after(parts[1], *bases))
        received[0] = after(received[0], *bases, *waits)
        if step == 0:
            w_other = other_projection(piece, parts[1], w_out.shape)
        if step < STEPS - 1:
            new = []
            for n in range(CHUNKS):
                block = kernel_call(
                    project_kernel,
                    (count, 2 * width),
                    (level_index,),
                    (*table, w_other, bases[n], after(received[n], *new)),
                    out_products,
                )
                new.append(block)
            state = (fresh[step], fresh_other, *[down(block) for block in new])
            near_kind, near = "chunks", [after(block, state[2]) for block in new]
            kind = "fresh"
        else:
            done = []
            for n in range(CHUNKS):
                pair = kernel_call(
                    functools.partial(final_kernel, kind, n * count),
                    ((count, width), (count, width)),
                    (level_index,),
                    (rows_mine, w_other, bases[n], after(received[n], *(p[0] for p in done)), *state),
                    out_products // 2,
                )
                done.append(pair)
            advanced = [down(block) for block, _ in done]
            first = kernel_call(enter_kernel, (count, width), (), (advanced[0], fresh[step]))
            final, velocity = kernel_call(
                finish_kernel,
                ((rows, width), (rows, width)),
                (),
                (first, after(advanced[1], first), fresh[step], done[0][1], done[1][1]),
            )
    return (final, velocity)


def solution(mesh):
    placed = (
        P("queue", "heads"),
        P(None, None, "heads"),
        P(),
        P(),
        P(None, "heads"),
        P(None, "heads"),
        P(None, "heads"),
        P(None, None, "heads"),
        P("heads"),
        P("heads"),
        P("heads", None),
    )
    return jax.shard_map(
        on_device,
        mesh=mesh,
        in_specs=placed,
        out_specs=(P("queue", "heads"), P("queue", "heads")),
        check_vma=False,
    )
```
